256 devices in a mesh: ctx: 32 (over y, x, core), tp: 8 (over z).
Axes of the slice: x: 4, y: 4, z: 8, core: 2. Of those that a mesh axis runs over, the one named last changes fastest.
Arguments:
- token_ids: int32 [8192], P('ctx'), may hold values from 0 to 511
- table: bfloat16 [512, 3, 4096], P(None, None, 'tp'), may hold values from -6 to 6
- filter_raw: float32 [8192, 4096], P('ctx', 'tp'), may hold values from -6 to 6
- w_out: bfloat16 [4096, 4096], P('tp'), may hold values from -0.09375 to 0.09375
- cotangent: bfloat16 [8192, 4096], P('ctx', 'tp'), may hold values from -6 to 6
Outputs:
- output: bfloat16 [8192, 4096], P('ctx', 'tp')
- grad_filter: float32 [8192, 4096], P('ctx', 'tp')
- grad_table: float32 [512, 3, 4096], P('ctx', None, 'tp')
The draws below stay inside these ranges and needn't reach their ends.
All inputs are finite; a program needn't handle non-finite values.
Results may differ from the reference program's by a relative error of at most 0.019.
Values may be sent and summed in bfloat16 or wider, within the bound.
No kernel may reach another device: no remote copies, remote signals or barrier semaphores. Data moves between devices by JAX's collectives and lax.ppermute only.
A program may use at most 128 MiB of HBM per device.

```python
import jax
import jax.numpy as jnp
from jax import lax

C = 4096
V = 512
L = 8192


def place_ends(values, rng, least, largest):
    dims = values.shape
    place = [jax.random.randint(jax.random.fold_in(rng, axis), (), 0, dims[axis]) for axis in range(len(dims))]
    values = values.at[tuple(place)].set(least)
    longest = dims.index(max(dims))
    place[longest] = (place[longest] + 1) % dims[longest]
    return values.at[tuple(place)].set(largest)


def shard_levels(stream_key, dims, pieces, low, high):
    factor_of = 1.0
    for position, parts in pieces:
        steps = jax.random.uniform(jax.random.fold_in(jax.random.fold_in(stream_key, 6), position), (parts,), jnp.float32, low / len(pieces), high / len(pieces))
        factor_of = factor_of * jnp.repeat(jnp.exp(steps), dims[position] // parts).reshape((-1,) + (1,) * (len(dims) - 1 - position))
    return factor_of


def normal_values(stream_key, shape, scale, most, cuts=(), held_as=jnp.bfloat16):
    factor_of = shard_levels(stream_key, shape, cuts, -0.22, 0.18) if cuts else 1.0
    values = jax.random.normal(stream_key, shape, jnp.float32) * scale * factor_of
    return jnp.minimum(jnp.maximum(values, -most), most).astype(held_as)


def setup_inputs(seed: int = 0) -> dict:
    key_of = jax.random.split(jax.random.key(seed), 6)
    token_ids = place_ends(jax.random.randint(key_of[0], (L,), 0, V), jax.random.fold_in(key_of[0], 1), 0, V - 1).astype(jnp.int32)
    table = normal_values(key_of[1], (V, 3, C), 1.0, 6.0, ((2, 8),))
    filter_raw = normal_values(key_of[2], (L, C), 1.0, 6.0, ((0, 32), (1, 8)), jnp.float32)
    w_out = normal_values(key_of[3], (C, C), C ** -0.5, 0.09375, ((0, 8),))
    cotangent = normal_values(key_of[4], (L, C), 1.0, 6.0, ((0, 32), (1, 8)))
    return dict(token_ids=token_ids, table=table, filter_raw=filter_raw, w_out=w_out, cotangent=cotangent)


def blockwise(function, *fields):
    total_len, width = fields[0].shape
    step_width = min(width, 256)
    stacked = tuple((jnp.moveaxis(member.reshape(total_len, width // step_width, step_width), 1, 0) for member in fields))
    result = lax.map(lambda grouped: function(*grouped), stacked)
    return jnp.moveaxis(result, 0, 1).reshape(total_len, width)

def causal_product(signal, kernel):
    period = 2 * signal.shape[0]
    spectrum = jnp.fft.rfft(signal, n=period, axis=0) * jnp.fft.rfft(kernel, n=period, axis=0)
    return jnp.fft.irfft(spectrum, n=period, axis=0)[:signal.shape[0]]

def correlate(kernel, signal):
    period = 2 * signal.shape[0]
    spectrum = jnp.conj(jnp.fft.rfft(kernel, n=period, axis=0)) * jnp.fft.rfft(signal, n=period, axis=0)
    return jnp.fft.irfft(spectrum, n=period, axis=0)[:signal.shape[0]]

def reference(token_ids, table, filter_raw, w_out, cotangent):
    embedded = jnp.take(table, token_ids, axis=0)
    query_part = embedded[:, 0].astype(jnp.float32)
    key_part = embedded[:, 1].astype(jnp.float32)
    value_part = embedded[:, 2].astype(jnp.float32)
    gated_input = key_part * value_part
    filter_scale = 1.0 / jnp.sqrt(jnp.float32(L))
    kernel = filter_raw * filter_scale
    causal = blockwise(causal_product, gated_input, kernel)
    mixed_rows = (query_part * causal).astype(jnp.bfloat16)
    output = jnp.dot(mixed_rows, w_out, preferred_element_type=jnp.float32).astype(jnp.bfloat16)
    back_grad = jnp.dot(cotangent, w_out.T, preferred_element_type=jnp.float32)
    causal_grad = back_grad * query_part
    query_grad = back_grad * causal
    gated_grad = blockwise(correlate, kernel, causal_grad)
    filter_grad = blockwise(correlate, gated_input, causal_grad)
    grad_filter = filter_grad * filter_scale
    activation = jnp.stack([query_grad, gated_grad * value_part, gated_grad * key_part], axis=1).astype(jnp.bfloat16)
    grad_table = jax.ops.segment_sum(activation.astype(jnp.float32), token_ids, num_segments=V)
    return (output, grad_filter, grad_table)
```

```python
import functools
import math

import jax
import jax.numpy as jnp
import ml_dtypes
import numpy as np
from jax import lax
from jax.experimental import pallas as pl
from jax.experimental.pallas import tpu as pltpu
from jax.sharding import PartitionSpec as P

BF = jnp.bfloat16
F32 = jnp.float32


def split_np(values):
    high = values.astype(np.float32).astype(ml_dtypes.bfloat16)
    low = (values - high.astype(np.float64)).astype(np.float32).astype(ml_dtypes.bfloat16)
    return high, low


@functools.lru_cache(maxsize=None)
def tables(blocks, chans, rows):
    period = 2 * blocks * rows
    s = np.arange(blocks, dtype=np.float64)
    r = np.arange(rows, dtype=np.float64)
    odd = np.arange(blocks, dtype=np.float64) + 0.5
    outer = 2 * np.pi * odd[:, None] * s[None, :] / (2 * blocks)
    eye = np.eye(chans)
    real = np.einsum("ks,cd->cksd", np.cos(outer), eye).reshape(chans * blocks, blocks * chans)
    imag = np.einsum("ks,cd->cksd", -np.sin(outer), eye).reshape(chans * blocks, blocks * chans)
    first = np.concatenate([real, imag], axis=0)
    inner = 2 * np.pi * (np.outer(r, r) % rows) / rows
    cosine, sine = np.cos(inner), np.sin(inner)
    second = np.block([[cosine, -sine], [sine, cosine]])
    twist = 2 * np.pi * odd[:, None] * r[None, :] / period
    return (
        split_np(first),
        split_np(second),
        split_np(second.T.copy()),
        split_np(first.T * (2.0 / period)),
        np.cos(twist).astype(np.float32),
        np.sin(twist).astype(np.float32),
    )


def split(values):
    high = values.astype(BF)
    return high, (values - high.astype(F32)).astype(BF)


def mm(left, right):
    return jnp.dot(left, right, preferred_element_type=F32)


def twiddle(real, imag, cos_ref, sin_ref, sign):
    rows, lanes = real.shape
    blocks = cos_ref.shape[0]
    shape = (rows // blocks, blocks, lanes)
    cosine = cos_ref[...][None]
    sine = sin_ref[...][None] * sign
    real = real.reshape(shape)
    imag = imag.reshape(shape)
    return (
        (real * cosine + imag * sine).reshape(rows, lanes),
        (imag * cosine - real * sine).reshape(rows, lanes),
    )


def forward(high, low, first, second, cos_ref, sin_ref):
    first_high, first_low = first
    second_high, second_low = second
    stage = mm(first_high[...], high) + mm(first_low[...], high)
    if low is not None:
        stage = stage + mm(first_high[...], low)
    half = stage.shape[0] // 2
    real, imag = twiddle(stage[:half], stage[half:], cos_ref, sin_ref, 1.0)
    high, low = split(jnp.concatenate([real, imag], axis=1))
    return mm(high, second_high[...]) + mm(low, second_high[...]) + mm(high, second_low[...])


def inverse(spectrum, third, fourth, cos_ref, sin_ref):
    third_high, third_low = third
    fourth_high, fourth_low = fourth
    high, low = split(spectrum)
    stage = mm(high, third_high[...]) + mm(low, third_high[...]) + mm(high, third_low[...])
    half = stage.shape[1] // 2
    real, imag = twiddle(stage[:, :half], stage[:, half:], cos_ref, sin_ref, -1.0)
    high, low = split(jnp.concatenate([real, imag], axis=0))
    return mm(fourth_high[...], high) + mm(fourth_high[...], low) + mm(fourth_low[...], high)


def embed_kernel(ids_ref, tab_ref, q_ref, k_ref, v_ref):
    blocks, rows = ids_ref.shape
    chans = tab_ref.shape[0] // 3
    vocab = tab_ref.shape[1]
    labels = lax.broadcasted_iota(jnp.int32, (vocab, rows), 0)

    def body(s, carry):
        onehot = (labels == ids_ref[pl.ds(s, 1), :]).astype(F32).astype(BF)
        picked = mm(tab_ref[...], onehot).astype(BF)
        place = pl.ds(pl.multiple_of(s * chans, chans), chans)
        q_ref[place, :] = picked[:chans]
        k_ref[place, :] = picked[chans : 2 * chans]
        v_ref[place, :] = picked[2 * chans :]
        return carry

    lax.fori_loop(0, blocks, body, 0)


def input_kernel(k_ref, v_ref, first_high, first_low, second_high, second_low, cos_ref, sin_ref, spec_ref):
    gated = k_ref[...].astype(F32) * v_ref[...].astype(F32)
    high, low = split(gated)
    spec_ref[...] = forward(
        high, low, (first_high, first_low), (second_high, second_low), cos_ref, sin_ref
    )


def causal_kernel(
    scale, f_ref, q_ref, gated_ref,
    first_high, first_low, second_high, second_low,
    third_high, third_low, fourth_high, fourth_low, cos_ref, sin_ref,
    spec_ref, causal_ref, mixed_ref,
):
    spec = forward(
        f_ref[...], None, (first_high, first_low), (second_high, second_low), cos_ref, sin_ref
    ) * scale
    spec_ref[...] = spec
    half = spec.shape[1] // 2
    fr, fi = spec[:, :half], spec[:, half:]
    gr, gi = gated_ref[:, :half], gated_ref[:, half:]
    product = jnp.concatenate([gr * fr - gi * fi, gr * fi + gi * fr], axis=1)
    causal = inverse(
        product, (third_high, third_low), (fourth_high, fourth_low), cos_ref, sin_ref
    )
    causal_ref[...] = causal
    mixed_ref[...] = (q_ref[...].astype(F32) * causal).astype(BF)


def grad_kernel(
    scale, b_ref, q_ref, k_ref, v_ref, causal_ref, filter_ref, gated_ref,
    first_high, first_low, second_high, second_low,
    third_high, third_low, fourth_high, fourth_low, cos_ref, sin_ref,
    gf_ref, act_ref, spec_ref,
):
    back = b_ref[...].astype(F32)
    high, low = split(back * q_ref[...].astype(F32))
    spec_ref[...] = forward(
        high, low, (first_high, first_low), (second_high, second_low), cos_ref, sin_ref
    )
    half = spec_ref.shape[1] // 2

    def correlate(other_ref):
        cr, ci = spec_ref[:, :half], spec_ref[:, half:]
        xr, xi = other_ref[:, :half], other_ref[:, half:]
        product = jnp.concatenate([xr * cr + xi * ci, xr * ci - xi * cr], axis=1)
        return inverse(
            product, (third_high, third_low), (fourth_high, fourth_low), cos_ref, sin_ref
        )

    gf_ref[...] = (correlate(gated_ref) * scale).astype(BF)
    gated_grad = correlate(filter_ref)
    act_ref[0] = (back * causal_ref[...]).astype(BF)
    act_ref[1] = (gated_grad * v_ref[...].astype(F32)).astype(BF)
    act_ref[2] = (gated_grad * k_ref[...].astype(F32)).astype(BF)


def rows_kernel(ids_ref, act_ref, out_ref, acc_ref):
    blocks, rows = ids_ref.shape
    vocab = out_ref.shape[0]
    chans = act_ref.shape[1] // blocks
    labels = lax.broadcasted_iota(jnp.int32, (vocab, rows), 0)
    acc_ref[...] = jnp.zeros_like(acc_ref)

    def body(s, carry):
        onehot = (labels == ids_ref[pl.ds(s, 1), :]).astype(F32).astype(BF)
        place = pl.ds(pl.multiple_of(s * chans, chans), chans)
        act = jnp.concatenate([act_ref[j, place, :] for j in range(3)], axis=0)
        acc_ref[...] += lax.dot_general(
            onehot, act, (((1,), (1,)), ((), ())), preferred_element_type=F32
        )
        return carry

    lax.fori_loop(0, blocks, body, 0)
    out_ref[...] = acc_ref[...].astype(BF)


PARAMS = pltpu.CompilerParams(vmem_limit_bytes=48 * 1024 * 1024)


def shards(token_ids, table, filter_raw, w_out, cotangent):
    rows = token_ids.shape[0]
    blocks = lax.axis_size("ctx")
    width = filter_raw.shape[1]
    chans = width // blocks
    vocab = table.shape[0]
    length = rows * blocks
    position = lax.axis_index("ctx")
    scale = 1.0 / math.sqrt(length)
    first, second, third, fourth, cosine, sine = tables(blocks, chans, rows)
    field = jax.ShapeDtypeStruct((blocks * chans, rows), BF)
    wide = jax.ShapeDtypeStruct((blocks * chans, 2 * rows), F32)
    forward_args = (*first, *second)
    inverse_args = (*third, *fourth)

    def exchange(values):
        return lax.all_to_all(values, "ctx", split_axis=0, concat_axis=0, tiled=True)

    ids = lax.all_gather(token_ids, "ctx", axis=0, tiled=False)
    filter_field = exchange(filter_raw.astype(BF).T)
    cot_full = lax.all_gather(cotangent, "tp", axis=1, tiled=True)

    local = lax.dynamic_slice(table, (0, 0, position * chans), (vocab, 3, chans))
    local = local.transpose(1, 2, 0).reshape(3 * chans, vocab)
    query, key, value = pl.pallas_call(
        embed_kernel, out_shape=(field, field, field), compiler_params=PARAMS, name="embed"
    )(ids, local)
    gated_spec = pl.pallas_call(
        input_kernel, out_shape=wide, compiler_params=PARAMS, name="gated_spectrum"
    )(key, value, *forward_args, cosine, sine)
    filter_spec, causal, mixed = pl.pallas_call(
        functools.partial(causal_kernel, scale),
        out_shape=(wide, jax.ShapeDtypeStruct(field.shape, F32), field),
        compiler_params=PARAMS,
        name="causal",
    )(filter_field, query, gated_spec, *forward_args, *inverse_args, cosine, sine)
    mixed_rows = exchange(mixed)
    partial_out = lax.dot_general(
        mixed_rows, w_out, (((0,), (0,)), ((), ())), preferred_element_type=F32
    )
    output = lax.psum_scatter(partial_out.astype(BF), "tp", scatter_dimension=1, tiled=True)

    back = lax.dot_general(
        w_out, cot_full, (((1,), (1,)), ((), ())), preferred_element_type=F32
    )
    back_field = exchange(back.astype(BF))
    filter_grad, act = pl.pallas_call(
        functools.partial(grad_kernel, scale),
        out_shape=(field, jax.ShapeDtypeStruct((3,) + field.shape, BF)),
        scratch_shapes=[pltpu.VMEM(wide.shape, F32)],
        compiler_params=PARAMS,
        name="grads",
    )(
        back_field, query, key, value, causal, filter_spec, gated_spec,
        *forward_args, *inverse_args, cosine, sine,
    )
    grad_filter = exchange(filter_grad).T.astype(F32)
    row_sums = pl.pallas_call(
        rows_kernel,
        out_shape=jax.ShapeDtypeStruct((vocab, 3 * chans), BF),
        scratch_shapes=[pltpu.VMEM((vocab, 3 * chans), F32)],
        compiler_params=PARAMS,
        name="row_sums",
    )(ids, act)
    grad_rows = exchange(row_sums)
    vocab_rows = vocab // blocks
    grad_rows = grad_rows.reshape(blocks, vocab_rows, 3, chans).transpose(1, 2, 0, 3)
    grad_table = grad_rows.reshape(vocab_rows, 3, width).astype(F32)
    return (output, grad_filter, grad_table)


def solution(mesh):
    return jax.shard_map(
        shards,
        mesh=mesh,
        in_specs=(P("ctx"), P(None, None, "tp"), P("ctx", "tp"), P("tp", None), P("ctx", "tp")),
        out_specs=(P("ctx", "tp"), P("ctx", "tp"), P("ctx", None, "tp")),
        check_vma=False,
    )
```

```python
import functools
import math

import jax
import jax.numpy as jnp
import ml_dtypes
import numpy as np
from jax import lax
from jax.experimental import pallas as pl
from jax.experimental.pallas import tpu as pltpu
from jax.sharding import PartitionSpec as P

BF = jnp.bfloat16
F32 = jnp.float32


def split_np(values):
    high = values.astype(np.float32).astype(ml_dtypes.bfloat16)
    low = (values - high.astype(np.float64)).astype(np.float32).astype(ml_dtypes.bfloat16)
    return high, low


@functools.lru_cache(maxsize=None)
def tables(blocks, chans, rows):
    period = 2 * blocks * rows
    s = np.arange(blocks, dtype=np.float64)
    r = np.arange(rows, dtype=np.float64)
    odd = np.arange(blocks, dtype=np.float64) + 0.5
    outer = 2 * np.pi * odd[:, None] * s[None, :] / (2 * blocks)
    eye = np.eye(chans)
    real = np.einsum("ks,cd->cksd", np.cos(outer), eye).reshape(chans * blocks, blocks * chans)
    imag = np.einsum("ks,cd->cksd", -np.sin(outer), eye).reshape(chans * blocks, blocks * chans)
    first = np.concatenate([real, imag], axis=0)
    inner = 2 * np.pi * (np.outer(r, r) % rows) / rows
    cosine, sine = np.cos(inner), np.sin(inner)
    second = np.block([[cosine, -sine], [sine, cosine]])
    twist = 2 * np.pi * odd[:, None] * r[None, :] / period
    return (
        *split_np(first),
        *split_np(second),
        *split_np(second.T.copy()),
        *split_np(first.T * (2.0 / period)),
        np.cos(twist).astype(np.float32),
        np.sin(twist).astype(np.float32),
    )


def split(values):
    high = values.astype(BF)
    return high, (values - high.astype(F32)).astype(BF)


def mm(left, right):
    return jnp.dot(left, right, preferred_element_type=F32)


def twiddle(real, imag, cos_ref, sin_ref, sign):
    rows, lanes = real.shape
    blocks = cos_ref.shape[0]
    shape = (rows // blocks, blocks, lanes)
    cosine = cos_ref[...][None]
    sine = sin_ref[...][None] * sign
    real = real.reshape(shape)
    imag = imag.reshape(shape)
    return (
        (real * cosine + imag * sine).reshape(rows, lanes),
        (imag * cosine - real * sine).reshape(rows, lanes),
    )


def forward(values, low_too, constants):
    first_high, first_low, second_high, second_low = constants[:4]
    cos_ref, sin_ref = constants[8:]
    high, low = split(values)
    stage = mm(first_high[...], high) + mm(first_low[...], high)
    if low_too:
        stage = stage + mm(first_high[...], low)
    half = stage.shape[0] // 2
    real, imag = twiddle(stage[:half], stage[half:], cos_ref, sin_ref, 1.0)
    high, low = split(jnp.concatenate([real, imag], axis=1))
    return mm(high, second_high[...]) + mm(low, second_high[...]) + mm(high, second_low[...])


def inverse(real, imag, constants):
    third_high, third_low, fourth_high, fourth_low, cos_ref, sin_ref = constants[4:]
    high, low = split(jnp.concatenate([real, imag], axis=1))
    stage = mm(high, third_high[...]) + mm(low, third_high[...]) + mm(high, third_low[...])
    half = stage.shape[1] // 2
    real, imag = twiddle(stage[:, :half], stage[:, half:], cos_ref, sin_ref, -1.0)
    high, low = split(jnp.concatenate([real, imag], axis=0))
    return mm(fourth_high[...], high) + mm(fourth_high[...], low) + mm(fourth_low[...], high)


def spread(values, wide_ref):
    wide_ref[...] = values.reshape(wide_ref.shape)


def group_of(wide_ref, group):
    blocks, _, size, lanes = wide_ref.shape
    return wide_ref[:, group].reshape(blocks * size, lanes)


def joined(wide_ref):
    blocks, groups, size, lanes = wide_ref.shape
    return wide_ref[...].reshape(blocks * groups * size, lanes)


def fetch(sources, targets, sems):
    copies = [
        pltpu.make_async_copy(source, target, sems.at[place])
        for place, (source, target) in enumerate(zip(sources, targets))
    ]
    for copy in copies:
        copy.start()
    return copies


def wait_all(copies):
    for copy in copies:
        copy.wait()


def onehots(ids_ref, s, chans, vocab):
    quarter = chans // 4
    lanes = ids_ref.shape[1]
    block = ids_ref[pl.ds(pl.multiple_of(s * chans, chans), chans), :]
    block = block.astype(F32)
    labels = lax.broadcasted_iota(jnp.int32, (16, lanes), 0).astype(F32)
    halves = []
    for half in range(2):
        coarse = jnp.broadcast_to(block[half * quarter : half * quarter + 1], (16, lanes))
        fine = block[(2 + half) * quarter : (2 + half) * quarter + 1]
        fine_hot = (labels == fine).astype(F32).astype(BF)
        coarse = coarse.astype(BF)
        zero = jnp.zeros_like(fine_hot)
        halves.append(
            jnp.concatenate(
                [
                    jnp.where(coarse == jnp.array(part, BF), fine_hot, zero)
                    for part in range(vocab // 16)
                ],
                axis=0,
            )
        )
    return jnp.concatenate(halves, axis=1)


def send_kernel(f_ref, ids_ref, out_ref):
    rows, width = f_ref.shape
    out_ref[:, :rows] = f_ref[...].T.astype(BF)
    ids = ids_ref[...]
    coarse = ids // 16
    pieces = (coarse, ids - 16 * coarse)
    lanes = 128
    quarters = [
        jnp.broadcast_to(piece[:, half * lanes : (half + 1) * lanes].astype(F32), (4, lanes))
        for piece in pieces
        for half in range(2)
    ]
    tile = jnp.concatenate(quarters, axis=0).astype(BF)
    for start in range(0, width, 16):
        out_ref[start : start + 16, rows:] = tile


def front_kernel(
    scale, in_ref, tab_ref, *refs,
):
    constants_hbm, refs = refs[:10], refs[10:]
    outs, refs = refs[:7], refs[7:]
    mixed_ref, refs = refs[0], refs[1:]
    constants, refs = refs[:10], refs[10:]
    held, refs = refs[:7], refs[7:]
    wide_ref, in_sems, out_sems = refs
    q_ref, k_ref, v_ref, ids_ref, filter_ref, gated_ref, causal_ref = held
    incoming = fetch(constants_hbm, constants, in_sems)
    rows = q_ref.shape[1]
    chans = tab_ref.shape[0] // 3
    vocab = tab_ref.shape[1]
    blocks = q_ref.shape[0] // chans
    part = q_ref.shape[0] // 2

    def leave(first, last):
        copies = [
            pltpu.make_async_copy(held[place], outs[place], out_sems.at[place])
            for place in range(first, last)
        ]
        for copy in copies:
            copy.start()
        return copies

    ids_ref[...] = in_ref[:, rows:]

    def body(s, carry):
        picked = mm(tab_ref[...], onehots(ids_ref, s, chans, vocab)).astype(BF)
        place = pl.ds(pl.multiple_of(s * chans, chans), chans)
        q_ref[place, :] = picked[:chans]
        k_ref[place, :] = picked[chans : 2 * chans]
        v_ref[place, :] = picked[2 * chans :]
        return carry

    lax.fori_loop(0, blocks, body, 0, unroll=2)
    leaving = leave(0, 4)
    wait_all(incoming)
    spread(in_ref[:, :rows].astype(F32), wide_ref)
    for group in range(2):
        place = slice(group * part, (group + 1) * part)
        filter_ref[place] = forward(group_of(wide_ref, group), False, constants) * scale
    leaving += leave(4, 5)
    spread(k_ref[...].astype(F32) * v_ref[...].astype(F32), wide_ref)
    for group in range(2):
        place = slice(group * part, (group + 1) * part)
        gated_ref[place] = forward(group_of(wide_ref, group), True, constants)
    leaving += leave(5, 6)
    size = wide_ref.shape[2]
    for group in range(2):
        place = slice(group * part, (group + 1) * part)
        fr, fi = filter_ref[place, :rows], filter_ref[place, rows:]
        gr, gi = gated_ref[place, :rows], gated_ref[place, rows:]
        causal = inverse(gr * fr - gi * fi, gr * fi + gi * fr, constants)
        wide_ref[:, group] = causal.reshape(blocks, size, rows)
    causal = joined(wide_ref)
    causal_ref[...] = causal
    leaving += leave(6, 7)
    mixed_ref[...] = (q_ref[...].astype(F32) * causal).astype(BF)
    wait_all(leaving)


def back_kernel(scale, b_ref, *refs):
    sources, refs = refs[:17], refs[17:]
    out_ref, refs = refs[0], refs[1:]
    held, refs = refs[:17], refs[17:]
    act_ref, spec_ref, acc_ref, wide_ref, sems = refs
    incoming = fetch(sources, held, sems)
    constants, q_ref, causal_ref, gated_ref, filter_ref, k_ref, v_ref, ids_ref = (
        (*held[1:5], *held[8:12], *held[5:7]), held[0], held[12], held[7], *held[13:]
    )
    rows = b_ref.shape[1]
    blocks = act_ref.shape[0]
    chans = b_ref.shape[0] // blocks
    vocab = acc_ref.shape[0]
    part = b_ref.shape[0] // 2
    size = wide_ref.shape[2]
    shape = (blocks, chans, rows)
    wait_all(incoming[:7])
    spread(b_ref[...].astype(F32) * q_ref[...].astype(F32), wide_ref)
    for group in range(2):
        place = slice(group * part, (group + 1) * part)
        spec_ref[place] = forward(group_of(wide_ref, group), True, constants)

    def correlate(other_ref):
        for group in range(2):
            place = slice(group * part, (group + 1) * part)
            cr, ci = spec_ref[place, :rows], spec_ref[place, rows:]
            xr, xi = other_ref[place, :rows], other_ref[place, rows:]
            result = inverse(xr * cr + xi * ci, xr * ci - xi * cr, constants)
            wide_ref[:, group] = result.reshape(blocks, size, rows)
        return joined(wide_ref)

    wait_all(incoming[7:])
    out_ref[:, :rows] = (correlate(gated_ref) * scale).astype(BF)
    act_ref[:, :chans] = (b_ref[...].astype(F32) * causal_ref[...]).astype(BF).reshape(shape)
    gated_grad = correlate(filter_ref)
    act_ref[:, chans : 2 * chans] = (
        (gated_grad * v_ref[...].astype(F32)).astype(BF).reshape(shape)
    )
    act_ref[:, 2 * chans : 3 * chans] = (
        (gated_grad * k_ref[...].astype(F32)).astype(BF).reshape(shape)
    )
    act_ref[:, 3 * chans :] = jnp.zeros((blocks, 128 - 3 * chans, rows), BF)
    acc_ref[...] = jnp.zeros_like(acc_ref)
    group = 4

    def body(step, carry):
        hot = jnp.concatenate(
            [onehots(ids_ref, step * group + g, chans, vocab) for g in range(group)], axis=1
        )
        act = jnp.concatenate([act_ref[step * group + g] for g in range(group)], axis=1)
        acc_ref[...] += lax.dot_general(
            hot, act, (((1,), (1,)), ((), ())), preferred_element_type=F32
        )
        return carry

    lax.fori_loop(0, blocks // group, body, 0)
    out_ref[:, rows:] = acc_ref[...].astype(BF)


def finish_kernel(in_ref, grad_ref, table_ref):
    width, rows = grad_ref.shape[1], grad_ref.shape[0]
    vocab_rows = table_ref.shape[1]
    chans = vocab_rows * width // in_ref.shape[0]
    grad_ref[...] = in_ref[:, :rows].astype(F32).T
    sums = in_ref[:, rows:]
    lanes = sums.shape[1]
    column = lax.broadcasted_iota(jnp.int32, (lanes, width), 1)
    row = lax.broadcasted_iota(jnp.int32, (lanes, width), 0)
    source = lax.broadcasted_iota(jnp.int32, (width, width), 0) // vocab_rows
    mine = source == lax.broadcasted_iota(jnp.int32, (width, width), 1) // chans
    pick = lax.broadcasted_iota(jnp.int32, (vocab_rows, width), 1) % vocab_rows
    pick = pick == lax.broadcasted_iota(jnp.int32, (vocab_rows, width), 0)
    pick = pick.astype(F32).astype(BF)
    for field in range(3):
        take = (row == field * chans + column % chans).astype(F32).astype(BF)
        spreaded = jnp.where(mine, mm(sums, take), 0.0).astype(BF)
        table_ref[field] = mm(pick, spreaded)


def params(mebibytes):
    return pltpu.CompilerParams(vmem_limit_bytes=mebibytes * 1024 * 1024)


HBM = pl.BlockSpec(memory_space=pltpu.HBM)
VMEM = pl.BlockSpec(memory_space=pltpu.VMEM)


def scratch(arrays):
    return [pltpu.VMEM(array.shape, array.dtype) for array in arrays]


def shards(token_ids, table, filter_raw, w_out, cotangent):
    rows = token_ids.shape[0]
    blocks = lax.axis_size("ctx")
    width = filter_raw.shape[1]
    chans = width // blocks
    vocab = table.shape[0]
    length = rows * blocks
    position = lax.axis_index("ctx")
    scale = 1.0 / math.sqrt(length)
    constants = tables(blocks, chans // 2, rows)
    struct = jax.ShapeDtypeStruct
    field = struct((width, rows), BF)
    spectrum = struct((width, 2 * rows), F32)
    parcel = struct((width, rows + 128), BF)
    kept = (field, field, field, struct((width, 128), BF), spectrum, spectrum, struct(field.shape, F32))
    spread_shape = pltpu.VMEM((blocks, 2, chans // 2, rows), F32)

    def exchange(values):
        return lax.all_to_all(values, "ctx", split_axis=0, concat_axis=0, tiled=True)

    sent = pl.pallas_call(
        send_kernel, out_shape=parcel, compiler_params=params(62), name="send"
    )(filter_raw, token_ids[None])
    received = exchange(sent)
    cot_full = lax.all_gather(cotangent, "tp", axis=1, tiled=True)

    local = lax.dynamic_slice(table, (0, 0, position * chans), (vocab, 3, chans))
    local = local.transpose(1, 2, 0).reshape(3 * chans, vocab)
    query, key, value, ids, filter_spec, gated_spec, causal, mixed = pl.pallas_call(
        functools.partial(front_kernel, scale),
        out_shape=(*kept, field),
        in_specs=[VMEM, VMEM] + [HBM] * 10,
        out_specs=(HBM,) * 7 + (VMEM,),
        scratch_shapes=[
            *scratch(constants),
            *scratch(kept),
            spread_shape,
            pltpu.SemaphoreType.DMA((10,)),
            pltpu.SemaphoreType.DMA((7,)),
        ],
        compiler_params=params(62),
        name="front",
    )(received, local, *constants)
    mixed_rows = exchange(mixed)
    partial_out = lax.dot_general(
        mixed_rows, w_out, (((0,), (0,)), ((), ())), preferred_element_type=F32
    )
    output = lax.psum_scatter(partial_out.astype(BF), "tp", scatter_dimension=1, tiled=True)

    back = lax.dot_general(
        w_out, cot_full, (((1,), (1,)), ((), ())), preferred_element_type=F32
    )
    back_field = exchange(back.astype(BF))
    operands = (
        query, *constants[:4], *constants[8:], gated_spec, *constants[4:8], causal,
        filter_spec, key, value, ids,
    )
    grads = pl.pallas_call(
        functools.partial(back_kernel, scale),
        out_shape=parcel,
        in_specs=[VMEM] + [HBM] * 17,
        scratch_shapes=[
            *scratch(operands),
            pltpu.VMEM((blocks, 128, rows), BF),
            pltpu.VMEM(spectrum.shape, F32),
            pltpu.VMEM((vocab, 128), F32),
            spread_shape,
            pltpu.SemaphoreType.DMA((17,)),
        ],
        compiler_params=params(62),
        name="back",
    )(back_field, *operands)
    grads = exchange(grads)
    vocab_rows = vocab // blocks
    grad_filter, grad_table = pl.pallas_call(
        finish_kernel,
        out_shape=(struct((rows, width), F32), struct((3, vocab_rows, width), F32)),
        compiler_params=params(8),
        name="finish",
    )(grads)
    return (output, grad_filter, grad_table.transpose(1, 0, 2))


def solution(mesh):
    return jax.shard_map(
        shards,
        mesh=mesh,
        in_specs=(P("ctx"), P(None, None, "tp"), P("ctx", "tp"), P("tp", None), P("ctx", "tp")),
        out_specs=(P("ctx", "tp"), P("ctx", "tp"), P("ctx", None, "tp")),
        check_vma=False,
    )
```

```python
import functools
import math

import jax
import jax.numpy as jnp
import ml_dtypes
import numpy as np
from jax import lax
from jax.experimental import pallas as pl
from jax.experimental.pallas import tpu as pltpu
from jax.sharding import PartitionSpec as P

BF = jnp.bfloat16
F32 = jnp.float32


def split_np(values):
    high = values.astype(np.float32).astype(ml_dtypes.bfloat16)
    low = (values - high.astype(np.float64)).astype(np.float32).astype(ml_dtypes.bfloat16)
    return high, low


@functools.lru_cache(maxsize=None)
def tables(blocks, chans, rows):
    period = 2 * blocks * rows
    s = np.arange(blocks, dtype=np.float64)
    r = np.arange(rows, dtype=np.float64)
    odd = np.arange(blocks, dtype=np.float64) + 0.5
    outer = 2 * np.pi * odd[:, None] * s[None, :] / (2 * blocks)
    eye = np.eye(chans)
    real = np.einsum("ks,cd->cksd", np.cos(outer), eye).reshape(chans * blocks, blocks * chans)
    imag = np.einsum("ks,cd->cksd", -np.sin(outer), eye).reshape(chans * blocks, blocks * chans)
    first = np.concatenate([real, imag], axis=0)
    inner = 2 * np.pi * (np.outer(r, r) % rows) / rows
    cosine, sine = np.cos(inner), np.sin(inner)
    second = np.block([[cosine, -sine], [sine, cosine]])
    twist = 2 * np.pi * odd[:, None] * r[None, :] / period
    return np.concatenate(
        [
            np.concatenate(split_np(np.cos(twist)), axis=1),
            np.concatenate(split_np(np.sin(twist)), axis=1),
            np.concatenate(split_np(first), axis=1),
            *split_np(second),
            *split_np(second.T.copy()),
            *split_np(first.T * (2.0 / period)),
        ],
        axis=0,
    )


class Constants:
    def __init__(self, ref, blocks, rows):
        inner = ref.shape[1]
        start = 0

        def take(count):
            nonlocal start
            start += count
            return slice(start - count, start)

        cosine, sine, first = take(blocks), take(blocks), take(2 * rows)
        high, low = slice(0, rows), slice(rows, 2 * rows)
        self.cosine = lambda: ref[cosine, high].astype(F32) + ref[cosine, low].astype(F32)
        self.sine = lambda: ref[sine, high].astype(F32) + ref[sine, low].astype(F32)
        self.first = (ref.at[first, high], ref.at[first, low])
        self.second = (ref.at[take(inner)], ref.at[take(inner)])
        self.early = start
        self.third = (ref.at[take(inner)], ref.at[take(inner)])
        self.fourth = (ref.at[take(rows)], ref.at[take(rows)])


def split(values):
    high = values.astype(BF)
    return high, (values - high.astype(F32)).astype(BF)


def mm(left, right):
    return jnp.dot(left, right, preferred_element_type=F32)


def twiddle(real, imag, cosine, sine):
    rows, lanes = real.shape
    blocks = cosine.shape[0]
    shape = (rows // blocks, blocks, lanes)
    cosine = cosine[None]
    sine = sine[None]
    real = real.reshape(shape)
    imag = imag.reshape(shape)
    return (
        (real * cosine + imag * sine).reshape(rows, lanes),
        (imag * cosine - real * sine).reshape(rows, lanes),
    )


def forward(values, low_too, constants):
    first_high, first_low = constants.first
    second_high, second_low = constants.second
    high, low = split(values)
    stage = mm(first_high[...], high) + mm(first_low[...], high)
    if low_too:
        stage = stage + mm(first_high[...], low)
    half = stage.shape[0] // 2
    real, imag = twiddle(stage[:half], stage[half:], constants.cosine(), constants.sine())
    high, low = split(jnp.concatenate([real, imag], axis=1))
    return mm(high, second_high[...]) + mm(low, second_high[...]) + mm(high, second_low[...])


def inverse(real, imag, constants):
    third_high, third_low = constants.third
    fourth_high, fourth_low = constants.fourth
    high, low = split(jnp.concatenate([real, imag], axis=1))
    stage = mm(high, third_high[...]) + mm(low, third_high[...]) + mm(high, third_low[...])
    half = stage.shape[1] // 2
    real, imag = twiddle(stage[:, :half], stage[:, half:], constants.cosine(), -constants.sine())
    high, low = split(jnp.concatenate([real, imag], axis=0))
    return mm(fourth_high[...], high) + mm(fourth_high[...], low) + mm(fourth_low[...], high)


def spread(values, wide_ref):
    wide_ref[...] = values.reshape(wide_ref.shape)


def group_of(wide_ref, group):
    blocks, _, size, lanes = wide_ref.shape
    return wide_ref[:, group].reshape(blocks * size, lanes)


def joined(wide_ref):
    blocks, groups, size, lanes = wide_ref.shape
    return wide_ref[...].reshape(blocks * groups * size, lanes)


def started(copies):
    for copy in copies:
        copy.start()
    return copies


def onehots(ids_ref, s, chans, vocab):
    quarter = chans // 4
    lanes = ids_ref.shape[1]
    block = ids_ref[pl.ds(pl.multiple_of(s * chans, chans), chans), :]
    block = block.astype(F32)
    labels = lax.broadcasted_iota(jnp.int32, (16, lanes), 0).astype(F32)
    halves = []
    for half in range(2):
        coarse = jnp.broadcast_to(block[half * quarter : half * quarter + 1], (16, lanes))
        fine = block[(2 + half) * quarter : (2 + half) * quarter + 1]
        fine_hot = (labels == fine).astype(F32).astype(BF)
        coarse = coarse.astype(BF)
        zero = jnp.zeros_like(fine_hot)
        halves.append(
            jnp.concatenate(
                [
                    jnp.where(coarse == jnp.array(part, BF), fine_hot, zero)
                    for part in range(vocab // 16)
                ],
                axis=0,
            )
        )
    return jnp.concatenate(halves, axis=1)


def send_kernel(f_ref, ids_ref, out_ref):
    rows, width = f_ref.shape
    out_ref[:, :rows] = f_ref[...].T.astype(BF)
    ids = ids_ref[...]
    coarse = ids // 16
    pieces = (coarse, ids - 16 * coarse)
    lanes = 128
    quarters = [
        jnp.broadcast_to(piece[:, half * lanes : (half + 1) * lanes].astype(F32), (4, lanes))
        for piece in pieces
        for half in range(2)
    ]
    tile = jnp.concatenate(quarters, axis=0).astype(BF)
    for start in range(0, width, 16):
        out_ref[start : start + 16, rows:] = tile


def front_kernel(
    scale, in_ref, tab_ref, constants_hbm, parts_hbm, spectra_hbm, mixed_ref,
    constants_ref, parts_ref, spectra_ref, wide_ref, in_sems, out_sems,
):
    width, rows = mixed_ref.shape
    chans = tab_ref.shape[0] // 3
    vocab = tab_ref.shape[1]
    blocks = width // chans
    half = width // 2
    size = wide_ref.shape[2]
    constants = Constants(constants_ref, blocks, rows)
    total = constants_ref.shape[0]
    incoming = started(
        [
            pltpu.make_async_copy(constants_hbm.at[part], constants_ref.at[part], in_sems.at[place])
            for place, part in enumerate((slice(0, constants.early), slice(constants.early, total)))
        ]
    )
    query, key, value, ids = (slice(rows * part, rows * (part + 1)) for part in range(4))
    ids = slice(3 * rows, parts_ref.shape[1])
    parts_ref[:, ids] = in_ref[:, rows:]

    def body(s, carry):
        picked = mm(tab_ref[...], onehots(parts_ref.at[:, ids], s, chans, vocab)).astype(BF)
        place = pl.ds(pl.multiple_of(s * chans, chans), chans)
        parts_ref[place, query] = picked[:chans]
        parts_ref[place, key] = picked[chans : 2 * chans]
        parts_ref[place, value] = picked[2 * chans :]
        return carry

    lax.fori_loop(0, blocks, body, 0, unroll=8)
    leaving = started([pltpu.make_async_copy(parts_ref, parts_hbm, out_sems.at[0])])
    incoming[0].wait()
    spread(in_ref[:, :rows].astype(F32), wide_ref)
    fr, fi, gr, gi, cause = (slice(rows * part, rows * (part + 1)) for part in range(5))
    for group in range(2):
        place = slice(group * half, (group + 1) * half)
        spectra_ref[place, : 2 * rows] = forward(group_of(wide_ref, group), False, constants) * scale
    spread(parts_ref[:, key].astype(F32) * parts_ref[:, value].astype(F32), wide_ref)
    for group in range(2):
        place = slice(group * half, (group + 1) * half)
        spectra_ref[place, 2 * rows : 4 * rows] = forward(
            group_of(wide_ref, group), True, constants
        )
    leaving += started(
        [
            pltpu.make_async_copy(
                spectra_ref.at[:, : 4 * rows], spectra_hbm.at[:, : 4 * rows], out_sems.at[1]
            )
        ]
    )
    incoming[1].wait()
    for group in range(2):
        place = slice(group * half, (group + 1) * half)
        a, b = spectra_ref[place, fr], spectra_ref[place, fi]
        c, d = spectra_ref[place, gr], spectra_ref[place, gi]
        causal = inverse(c * a - d * b, c * b + d * a, constants)
        wide_ref[:, group] = causal.reshape(blocks, size, rows)
    causal = joined(wide_ref)
    spectra_ref[:, cause] = causal
    leaving += started(
        [
            pltpu.make_async_copy(
                spectra_ref.at[:, cause], spectra_hbm.at[:, cause], out_sems.at[2]
            )
        ]
    )
    mixed_ref[...] = (parts_ref[:, query].astype(F32) * causal).astype(BF)
    for copy in leaving:
        copy.wait()


def back_kernel(
    scale, b_ref, constants_ref, parts_ref, spectra_ref, out_ref,
    act_ref, spec_ref, acc_ref, wide_ref,
):
    width, rows = b_ref.shape
    blocks = act_ref.shape[0]
    chans = width // blocks
    vocab = acc_ref.shape[0]
    half = width // 2
    size = wide_ref.shape[2]
    shape = (blocks, chans, rows)
    constants = Constants(constants_ref, blocks, rows)
    query, key, value = (slice(rows * part, rows * (part + 1)) for part in range(3))
    ids = slice(3 * rows, parts_ref.shape[1])
    spread(b_ref[...].astype(F32) * parts_ref[:, query].astype(F32), wide_ref)
    for group in range(2):
        place = slice(group * half, (group + 1) * half)
        spec_ref[place] = forward(group_of(wide_ref, group), True, constants)

    def correlate(start):
        for group in range(2):
            place = slice(group * half, (group + 1) * half)
            cr, ci = spec_ref[place, :rows], spec_ref[place, rows:]
            xr = spectra_ref[place, start : start + rows]
            xi = spectra_ref[place, start + rows : start + 2 * rows]
            result = inverse(xr * cr + xi * ci, xr * ci - xi * cr, constants)
            wide_ref[:, group] = result.reshape(blocks, size, rows)
        return joined(wide_ref)

    out_ref[:, :rows] = (correlate(2 * rows) * scale).astype(BF)
    causal = spectra_ref[:, 4 * rows :]
    act_ref[:, :chans] = (b_ref[...].astype(F32) * causal).astype(BF).reshape(shape)
    gated_grad = correlate(0)
    act_ref[:, chans : 2 * chans] = (
        (gated_grad * parts_ref[:, value].astype(F32)).astype(BF).reshape(shape)
    )
    act_ref[:, 2 * chans :] = (
        (gated_grad * parts_ref[:, key].astype(F32)).astype(BF).reshape(shape)
    )
    acc_ref[...] = jnp.zeros_like(acc_ref)
    group = 4

    def body(step, carry):
        hot = jnp.concatenate(
            [onehots(parts_ref.at[:, ids], step * group + g, chans, vocab) for g in range(group)],
            axis=1,
        )
        act = jnp.concatenate([act_ref[step * group + g] for g in range(group)], axis=1)
        acc_ref[:, : 3 * chans] += lax.dot_general(
            hot, act, (((1,), (1,)), ((), ())), preferred_element_type=F32
        )
        return carry

    lax.fori_loop(0, blocks // group, body, 0)
    out_ref[:, rows:] = acc_ref[...].astype(BF)


def output_kernel(mixed_ref, w_hbm, out_hbm, w_ref, out_ref, in_sems, out_sems):
    chunks = w_ref.shape[0]
    lanes = w_ref.shape[2]
    incoming = started(
        [
            pltpu.make_async_copy(
                w_hbm.at[:, chunk * lanes : (chunk + 1) * lanes], w_ref.at[chunk], in_sems.at[chunk]
            )
            for chunk in range(chunks)
        ]
    )
    left = mixed_ref[...].astype(F32).T.astype(BF)
    leaving = []
    for chunk in range(chunks):
        incoming[chunk].wait()
        place = slice(chunk * lanes, (chunk + 1) * lanes)
        out_ref[:, place] = mm(left, w_ref[chunk]).astype(BF)
        leaving += started(
            [pltpu.make_async_copy(out_ref.at[:, place], out_hbm.at[:, place], out_sems.at[chunk])]
        )
    for copy in leaving:
        copy.wait()


def project_kernel(w_hbm, cot_hbm, back_ref, w_ref, cot_ref, acc_ref, w_sems, cot_sems):
    chunks = w_ref.shape[0]
    lanes = w_ref.shape[2]
    incoming = [
        (
            pltpu.make_async_copy(
                cot_hbm.at[:, chunk * lanes : (chunk + 1) * lanes],
                cot_ref.at[chunk],
                cot_sems.at[chunk],
            ),
            pltpu.make_async_copy(
                w_hbm.at[:, chunk * lanes : (chunk + 1) * lanes], w_ref.at[chunk], w_sems.at[chunk]
            ),
        )
        for chunk in range(chunks)
    ]
    for pair in incoming:
        started(pair)
    for chunk in range(chunks):
        for copy in incoming[chunk]:
            copy.wait()
        term = lax.dot_general(
            w_ref[chunk], cot_ref[chunk], (((1,), (1,)), ((), ())), preferred_element_type=F32
        )
        if chunk:
            term = acc_ref[...] + term
        if chunk < chunks - 1:
            acc_ref[...] = term
        else:
            back_ref[...] = term.astype(BF)


def finish_kernel(in_ref, grad_ref, table_ref):
    width, rows = grad_ref.shape[1], grad_ref.shape[0]
    vocab_rows = table_ref.shape[1]
    chans = vocab_rows * width // in_ref.shape[0]
    grad_ref[...] = in_ref[:, :rows].astype(F32).T
    sums = in_ref[:, rows:]
    lanes = sums.shape[1]
    column = lax.broadcasted_iota(jnp.int32, (lanes, width), 1)
    row = lax.broadcasted_iota(jnp.int32, (lanes, width), 0)
    source = lax.broadcasted_iota(jnp.int32, (width, width), 0) // vocab_rows
    mine = source == lax.broadcasted_iota(jnp.int32, (width, width), 1) // chans
    pick = lax.broadcasted_iota(jnp.int32, (vocab_rows, width), 1) % vocab_rows
    pick = pick == lax.broadcasted_iota(jnp.int32, (vocab_rows, width), 0)
    pick = pick.astype(F32).astype(BF)
    for field in range(3):
        take = (row == field * chans + column % chans).astype(F32).astype(BF)
        spreaded = jnp.where(mine, mm(sums, take), 0.0).astype(BF)
        table_ref[field] = mm(pick, spreaded)


def params(mebibytes):
    return pltpu.CompilerParams(vmem_limit_bytes=mebibytes * 1024 * 1024)


HBM = pl.BlockSpec(memory_space=pltpu.HBM)
VMEM = pl.BlockSpec(memory_space=pltpu.VMEM)
DMA = pltpu.SemaphoreType.DMA


def shards(token_ids, table, filter_raw, w_out, cotangent):
    rows = token_ids.shape[0]
    blocks = lax.axis_size("ctx")
    width, features = w_out.shape
    chans = width // blocks
    vocab = table.shape[0]
    length = rows * blocks
    position = lax.axis_index("ctx")
    scale = 1.0 / math.sqrt(length)
    constants = tables(blocks, chans // 2, rows)
    struct = jax.ShapeDtypeStruct
    field = struct((width, rows), BF)
    parts = struct((width, 3 * rows + 128), BF)
    spectra = struct((width, 5 * rows), F32)
    parcel = struct((width, rows + 128), BF)
    spread_shape = pltpu.VMEM((blocks, 2, chans // 2, rows), F32)
    chunks = 8
    lanes = features // chunks

    def exchange(values):
        return lax.all_to_all(values, "ctx", split_axis=0, concat_axis=0, tiled=True)

    sent = pl.pallas_call(
        send_kernel, out_shape=parcel, compiler_params=params(62), name="send"
    )(filter_raw, token_ids[None])
    received = exchange(sent)
    cot_full = lax.all_gather(cotangent, "tp", axis=1, tiled=True)

    local = lax.dynamic_slice(table, (0, 0, position * chans), (vocab, 3, chans))
    local = local.transpose(1, 2, 0).reshape(3 * chans, vocab)
    held, spectra_held, mixed = pl.pallas_call(
        functools.partial(front_kernel, scale),
        out_shape=(parts, spectra, field),
        in_specs=[VMEM, VMEM, HBM],
        out_specs=(HBM, HBM, VMEM),
        scratch_shapes=[
            pltpu.VMEM(constants.shape, BF),
            pltpu.VMEM(parts.shape, BF),
            pltpu.VMEM(spectra.shape, F32),
            spread_shape,
            DMA((2,)),
            DMA((3,)),
        ],
        compiler_params=params(50),
        name="front",
    )(received, local, constants)
    mixed_rows = exchange(mixed)
    partial_out = pl.pallas_call(
        output_kernel,
        out_shape=struct((rows, features), BF),
        in_specs=[VMEM, HBM],
        out_specs=HBM,
        scratch_shapes=[
            pltpu.VMEM((chunks, width, lanes), BF),
            pltpu.VMEM((rows, features), BF),
            DMA((chunks,)),
            DMA((chunks,)),
        ],
        compiler_params=params(61),
        name="project_out",
    )(mixed_rows, w_out)
    output = lax.psum_scatter(partial_out, "tp", scatter_dimension=1, tiled=True)

    back = pl.pallas_call(
        project_kernel,
        out_shape=field,
        in_specs=[HBM, HBM],
        scratch_shapes=[
            pltpu.VMEM((chunks, width, lanes), BF),
            pltpu.VMEM((chunks, rows, lanes), BF),
            pltpu.VMEM(field.shape, F32),
            DMA((chunks,)),
            DMA((chunks,)),
        ],
        compiler_params=params(54),
        name="project_back",
    )(w_out, cot_full)
    back_field = exchange(back)
    grads = pl.pallas_call(
        functools.partial(back_kernel, scale),
        out_shape=parcel,
        scratch_shapes=[
            pltpu.VMEM((blocks, 3 * chans, rows), BF),
            pltpu.VMEM((width, 2 * rows), F32),
            pltpu.VMEM((vocab, 128), F32),
            spread_shape,
        ],
        compiler_params=params(24),
        name="back",
    )(back_field, constants, held, spectra_held)
    grads = exchange(grads)
    vocab_rows = vocab // blocks
    grad_filter, grad_table = pl.pallas_call(
        finish_kernel,
        out_shape=(struct((rows, width), F32), struct((3, vocab_rows, width), F32)),
        compiler_params=params(8),
        name="finish",
    )(grads)
    return (output, grad_filter, grad_table.transpose(1, 0, 2))


def solution(mesh):
    return jax.shard_map(
        shards,
        mesh=mesh,
        in_specs=(P("ctx"), P(None, None, "tp"), P("ctx", "tp"), P("tp", None), P("ctx", "tp")),
        out_specs=(P("ctx", "tp"), P("ctx", "tp"), P("ctx", None, "tp")),
        check_vma=False,
    )
```

```python
import functools
import math

import jax
import jax.numpy as jnp
import ml_dtypes
import numpy as np
from jax import lax
from jax.experimental import pallas as pl
from jax.experimental.pallas import tpu as pltpu
from jax.sharding import PartitionSpec as P

BF = jnp.bfloat16
F32 = jnp.float32


def split_np(values):
    high = values.astype(np.float32).astype(ml_dtypes.bfloat16)
    low = (values - high.astype(np.float64)).astype(np.float32).astype(ml_dtypes.bfloat16)
    return high, low


@functools.lru_cache(maxsize=None)
def tables(blocks, chans, rows):
    period = 2 * blocks * rows
    s = np.arange(blocks, dtype=np.float64)
    r = np.arange(rows, dtype=np.float64)
    odd = np.arange(blocks, dtype=np.float64) + 0.5
    outer = 2 * np.pi * odd[:, None] * s[None, :] / (2 * blocks)
    eye = np.eye(chans)
    real = np.einsum("ks,cd->cksd", np.cos(outer), eye).reshape(chans * blocks, blocks * chans)
    imag = np.einsum("ks,cd->cksd", -np.sin(outer), eye).reshape(chans * blocks, blocks * chans)
    first = np.concatenate([real, imag], axis=0)
    inner = 2 * np.pi * (np.outer(r, r) % rows) / rows
    cosine, sine = np.cos(inner), np.sin(inner)
    second = np.block([[cosine, -sine], [sine, cosine]])
    twist = 2 * np.pi * odd[:, None] * r[None, :] / period
    return np.concatenate(
        [
            np.concatenate(split_np(np.cos(twist)), axis=1),
            np.concatenate(split_np(np.sin(twist)), axis=1),
            np.concatenate(split_np(first), axis=1),
            *split_np(second),
            *split_np(second.T.copy()),
            *split_np(first.T * (2.0 / period)),
        ],
        axis=0,
    )


class Constants:
    def __init__(self, ref, blocks, rows):
        inner = ref.shape[1]
        start = 0

        def take(count):
            nonlocal start
            start += count
            return slice(start - count, start)

        cosine, sine, first = take(blocks), take(blocks), take(2 * rows)
        high, low = slice(0, rows), slice(rows, 2 * rows)
        self.cosine = lambda: ref[cosine, high].astype(F32) + ref[cosine, low].astype(F32)
        self.sine = lambda: ref[sine, high].astype(F32) + ref[sine, low].astype(F32)
        self.first = (ref.at[first, high], ref.at[first, low])
        self.second = (ref.at[take(inner)], ref.at[take(inner)])
        self.early = start
        self.third = (ref.at[take(inner)], ref.at[take(inner)])
        self.fourth = (ref.at[take(rows)], ref.at[take(rows)])


def split(values):
    high = values.astype(BF)
    return high, (values - high.astype(F32)).astype(BF)


def mm(left, right):
    return jnp.dot(left, right, preferred_element_type=F32)


def twiddle(real, imag, cosine, sine):
    rows, lanes = real.shape
    blocks = cosine.shape[0]
    shape = (rows // blocks, blocks, lanes)
    cosine = cosine[None]
    sine = sine[None]
    real = real.reshape(shape)
    imag = imag.reshape(shape)
    return (
        (real * cosine + imag * sine).reshape(rows, lanes),
        (imag * cosine - real * sine).reshape(rows, lanes),
    )


def forward(values, low_too, constants):
    first_high, first_low = constants.first
    second_high, second_low = constants.second
    high, low = split(values)
    stage = mm(first_high[...], high) + mm(first_low[...], high)
    if low_too:
        stage = stage + mm(first_high[...], low)
    half = stage.shape[0] // 2
    real, imag = twiddle(stage[:half], stage[half:], constants.cosine(), constants.sine())
    high, low = split(jnp.concatenate([real, imag], axis=1))
    return mm(high, second_high[...]) + mm(low, second_high[...]) + mm(high, second_low[...])


def inverse(real, imag, constants):
    third_high, third_low = constants.third
    fourth_high, fourth_low = constants.fourth
    high, low = split(jnp.concatenate([real, imag], axis=1))
    stage = mm(high, third_high[...]) + mm(low, third_high[...]) + mm(high, third_low[...])
    half = stage.shape[1] // 2
    real, imag = twiddle(stage[:, :half], stage[:, half:], constants.cosine(), -constants.sine())
    high, low = split(jnp.concatenate([real, imag], axis=0))
    return mm(fourth_high[...], high) + mm(fourth_high[...], low) + mm(fourth_low[...], high)


def spread(values, wide_ref):
    wide_ref[...] = values.reshape(wide_ref.shape)


def group_of(wide_ref, group):
    blocks, _, size, lanes = wide_ref.shape
    return wide_ref[:, group].reshape(blocks * size, lanes)


def joined(wide_ref):
    blocks, groups, size, lanes = wide_ref.shape
    return wide_ref[...].reshape(blocks * groups * size, lanes)


def started(copies):
    for copy in copies:
        copy.start()
    return copies


def onehots(ids_ref, s, chans, vocab):
    quarter = chans // 4
    lanes = ids_ref.shape[1]
    block = ids_ref[pl.ds(pl.multiple_of(s * chans, chans), chans), :]
    block = block.astype(F32)
    labels = lax.broadcasted_iota(jnp.int32, (16, lanes), 0).astype(F32)
    halves = []
    for half in range(2):
        coarse = jnp.broadcast_to(block[half * quarter : half * quarter + 1], (16, lanes))
        fine = block[(2 + half) * quarter : (2 + half) * quarter + 1]
        fine_hot = (labels == fine).astype(F32).astype(BF)
        coarse = coarse.astype(BF)
        zero = jnp.zeros_like(fine_hot)
        halves.append(
            jnp.concatenate(
                [
                    jnp.where(coarse == jnp.array(part, BF), fine_hot, zero)
                    for part in range(vocab // 16)
                ],
                axis=0,
            )
        )
    return jnp.concatenate(halves, axis=1)


def send_kernel(f_ref, ids_ref, out_ref):
    rows, width = f_ref.shape
    out_ref[:, :rows] = f_ref[...].T.astype(BF)
    ids = ids_ref[...]
    coarse = ids // 16
    pieces = (coarse, ids - 16 * coarse)
    lanes = 128
    quarters = [
        jnp.broadcast_to(piece[:, half * lanes : (half + 1) * lanes].astype(F32), (4, lanes))
        for piece in pieces
        for half in range(2)
    ]
    tile = jnp.concatenate(quarters, axis=0).astype(BF)
    for start in range(0, width, 16):
        out_ref[start : start + 16, rows:] = tile


def front_kernel(
    scale, in_ref, tab_ref, constants_hbm, parts_hbm, spectra_hbm, mixed_ref,
    constants_ref, parts_ref, spectra_ref, wide_ref, in_sems, out_sems,
):
    width, rows = mixed_ref.shape
    chans = tab_ref.shape[0] // 3
    vocab = tab_ref.shape[1]
    blocks = width // chans
    half = width // 2
    size = wide_ref.shape[2]
    constants = Constants(constants_ref, blocks, rows)
    total = constants_ref.shape[0]
    incoming = started(
        [
            pltpu.make_async_copy(constants_hbm.at[part], constants_ref.at[part], in_sems.at[place])
            for place, part in enumerate((slice(0, constants.early), slice(constants.early, total)))
        ]
    )
    query, key, value, ids = (slice(rows * part, rows * (part + 1)) for part in range(4))
    ids = slice(3 * rows, parts_ref.shape[1])
    parts_ref[:, ids] = in_ref[:, rows:]

    def body(s, carry):
        picked = mm(tab_ref[...], onehots(in_ref.at[:, rows:], s, chans, vocab)).astype(BF)
        place = pl.ds(pl.multiple_of(s * chans, chans), chans)
        parts_ref[place, query] = picked[:chans]
        parts_ref[place, key] = picked[chans : 2 * chans]
        parts_ref[place, value] = picked[2 * chans :]
        return carry

    lax.fori_loop(0, blocks, body, 0, unroll=8)
    leaving = started([pltpu.make_async_copy(parts_ref, parts_hbm, out_sems.at[0])])
    incoming[0].wait()
    spread(in_ref[:, :rows].astype(F32), wide_ref)
    fr, fi, gr, gi, cause = (slice(rows * part, rows * (part + 1)) for part in range(5))
    for group in range(2):
        place = slice(group * half, (group + 1) * half)
        spectra_ref[place, : 2 * rows] = forward(group_of(wide_ref, group), False, constants) * scale
    spread(parts_ref[:, key].astype(F32) * parts_ref[:, value].astype(F32), wide_ref)
    for group in range(2):
        place = slice(group * half, (group + 1) * half)
        spectra_ref[place, 2 * rows : 4 * rows] = forward(
            group_of(wide_ref, group), True, constants
        )
    leaving += started(
        [
            pltpu.make_async_copy(
                spectra_ref.at[:, : 4 * rows], spectra_hbm.at[:, : 4 * rows], out_sems.at[1]
            )
        ]
    )
    incoming[1].wait()
    for group in range(2):
        place = slice(group * half, (group + 1) * half)
        a, b = spectra_ref[place, fr], spectra_ref[place, fi]
        c, d = spectra_ref[place, gr], spectra_ref[place, gi]
        causal = inverse(c * a - d * b, c * b + d * a, constants)
        wide_ref[:, group] = causal.reshape(blocks, size, rows)
    causal = joined(wide_ref)
    spectra_ref[:, cause] = causal
    leaving += started(
        [
            pltpu.make_async_copy(
                spectra_ref.at[:, cause], spectra_hbm.at[:, cause], out_sems.at[2]
            )
        ]
    )
    mixed_ref[...] = (parts_ref[:, query].astype(F32) * causal).astype(BF)
    for copy in leaving:
        copy.wait()


def back_kernel(
    scale, b_ref, constants_ref, parts_ref, spectra_ref, out_ref,
    act_ref, spec_ref, acc_ref, wide_ref,
):
    width, rows = b_ref.shape
    blocks = act_ref.shape[0]
    chans = width // blocks
    vocab = acc_ref.shape[0]
    half = width // 2
    size = wide_ref.shape[2]
    shape = (blocks, chans, rows)
    constants = Constants(constants_ref, blocks, rows)
    query, key, value = (slice(rows * part, rows * (part + 1)) for part in range(3))
    ids = slice(3 * rows, parts_ref.shape[1])
    spread(b_ref[...].astype(F32) * parts_ref[:, query].astype(F32), wide_ref)
    for group in range(2):
        place = slice(group * half, (group + 1) * half)
        spec_ref[place] = forward(group_of(wide_ref, group), True, constants)

    def correlate(start):
        for group in range(2):
            place = slice(group * half, (group + 1) * half)
            cr, ci = spec_ref[place, :rows], spec_ref[place, rows:]
            xr = spectra_ref[place, start : start + rows]
            xi = spectra_ref[place, start + rows : start + 2 * rows]
            result = inverse(xr * cr + xi * ci, xr * ci - xi * cr, constants)
            wide_ref[:, group] = result.reshape(blocks, size, rows)
        return joined(wide_ref)

    out_ref[:, :rows] = (correlate(2 * rows) * scale).astype(BF)
    causal = spectra_ref[:, 4 * rows :]
    act_ref[:, :chans] = (b_ref[...].astype(F32) * causal).astype(BF).reshape(shape)
    gated_grad = correlate(0)
    act_ref[:, chans : 2 * chans] = (
        (gated_grad * parts_ref[:, value].astype(F32)).astype(BF).reshape(shape)
    )
    act_ref[:, 2 * chans :] = (
        (gated_grad * parts_ref[:, key].astype(F32)).astype(BF).reshape(shape)
    )
    acc_ref[...] = jnp.zeros_like(acc_ref)
    group = 4

    def body(step, carry):
        hot = jnp.concatenate(
            [onehots(parts_ref.at[:, ids], step * group + g, chans, vocab) for g in range(group)],
            axis=1,
        )
        act = jnp.concatenate([act_ref[step * group + g] for g in range(group)], axis=1)
        acc_ref[:, : 3 * chans] += lax.dot_general(
            hot, act, (((1,), (1,)), ((), ())), preferred_element_type=F32
        )
        return carry

    lax.fori_loop(0, blocks // group, body, 0)
    out_ref[:, rows:] = acc_ref[...].astype(BF)


def finish_kernel(in_ref, grad_ref, table_ref):
    width, rows = grad_ref.shape[1], grad_ref.shape[0]
    vocab_rows = table_ref.shape[1]
    chans = vocab_rows * width // in_ref.shape[0]
    grad_ref[...] = in_ref[:, :rows].astype(F32).T
    sums = in_ref[:, rows:]
    lanes = sums.shape[1]
    column = lax.broadcasted_iota(jnp.int32, (lanes, width), 1)
    row = lax.broadcasted_iota(jnp.int32, (lanes, width), 0)
    source = lax.broadcasted_iota(jnp.int32, (width, width), 0) // vocab_rows
    mine = source == lax.broadcasted_iota(jnp.int32, (width, width), 1) // chans
    pick = lax.broadcasted_iota(jnp.int32, (vocab_rows, width), 1) % vocab_rows
    pick = pick == lax.broadcasted_iota(jnp.int32, (vocab_rows, width), 0)
    pick = pick.astype(F32).astype(BF)
    for field in range(3):
        take = (row == field * chans + column % chans).astype(F32).astype(BF)
        spreaded = jnp.where(mine, mm(sums, take), 0.0).astype(BF)
        table_ref[field] = mm(pick, spreaded)


def params(mebibytes):
    return pltpu.CompilerParams(vmem_limit_bytes=mebibytes * 1024 * 1024)


HBM = pl.BlockSpec(memory_space=pltpu.HBM)
VMEM = pl.BlockSpec(memory_space=pltpu.VMEM)
DMA = pltpu.SemaphoreType.DMA


def shards(token_ids, table, filter_raw, w_out, cotangent):
    rows = token_ids.shape[0]
    blocks = lax.axis_size("ctx")
    width, features = w_out.shape
    chans = width // blocks
    vocab = table.shape[0]
    length = rows * blocks
    position = lax.axis_index("ctx")
    scale = 1.0 / math.sqrt(length)
    constants = tables(blocks, chans // 2, rows)
    struct = jax.ShapeDtypeStruct
    field = struct((width, rows), BF)
    parts = struct((width, 3 * rows + 128), BF)
    spectra = struct((width, 5 * rows), F32)
    parcel = struct((width, rows + 128), BF)
    spread_shape = pltpu.VMEM((blocks, 2, chans // 2, rows), F32)
    chunks = 8
    lanes = features // chunks

    def exchange(values):
        return lax.all_to_all(values, "ctx", split_axis=0, concat_axis=0, tiled=True)

    sent = pl.pallas_call(
        send_kernel, out_shape=parcel, compiler_params=params(62), name="send"
    )(filter_raw, token_ids[None])
    received = exchange(sent)
    cot_full = lax.all_gather(cotangent, "tp", axis=1, tiled=True)

    local = lax.dynamic_slice(table, (0, 0, position * chans), (vocab, 3, chans))
    local = local.transpose(1, 2, 0).reshape(3 * chans, vocab)
    held, spectra_held, mixed = pl.pallas_call(
        functools.partial(front_kernel, scale),
        out_shape=(parts, spectra, field),
        in_specs=[VMEM, VMEM, HBM],
        out_specs=(HBM, HBM, VMEM),
        scratch_shapes=[
            pltpu.VMEM(constants.shape, BF),
            pltpu.VMEM(parts.shape, BF),
            pltpu.VMEM(spectra.shape, F32),
            spread_shape,
            DMA((2,)),
            DMA((3,)),
        ],
        compiler_params=params(50),
        name="front",
    )(received, local, constants)
    mixed_rows = exchange(mixed)
    partial_out = lax.dot_general(
        mixed_rows, w_out, (((0,), (0,)), ((), ())), preferred_element_type=F32
    ).astype(BF)
    output = lax.psum_scatter(partial_out, "tp", scatter_dimension=1, tiled=True)

    back = lax.dot_general(
        w_out, cot_full, (((1,), (1,)), ((), ())), preferred_element_type=F32
    ).astype(BF)
    back_field = exchange(back)
    grads = pl.pallas_call(
        functools.partial(back_kernel, scale),
        out_shape=parcel,
        scratch_shapes=[
            pltpu.VMEM((blocks, 3 * chans, rows), BF),
            pltpu.VMEM((width, 2 * rows), F32),
            pltpu.VMEM((vocab, 128), F32),
            spread_shape,
        ],
        compiler_params=params(24),
        name="back",
    )(back_field, constants, held, spectra_held)
    grads = exchange(grads)
    vocab_rows = vocab // blocks
    grad_filter, grad_table = pl.pallas_call(
        finish_kernel,
        out_shape=(struct((rows, width), F32), struct((3, vocab_rows, width), F32)),
        compiler_params=params(8),
        name="finish",
    )(grads)
    return (output, grad_filter, grad_table.transpose(1, 0, 2))


def solution(mesh):
    return jax.shard_map(
        shards,
        mesh=mesh,
        in_specs=(P("ctx"), P(None, None, "tp"), P("ctx", "tp"), P("tp", None), P("ctx", "tp")),
        out_specs=(P("ctx", "tp"), P("ctx", "tp"), P("ctx", None, "tp")),
        check_vma=False,
    )
```

```python
import functools
import math

import jax
import jax.numpy as jnp
import ml_dtypes
import numpy as np
from jax import lax
from jax.experimental import pallas as pl
from jax.experimental.pallas import tpu as pltpu
from jax.sharding import PartitionSpec as P

BF = jnp.bfloat16
F32 = jnp.float32


def split_np(values):
    high = values.astype(np.float32).astype(ml_dtypes.bfloat16)
    low = (values - high.astype(np.float64)).astype(np.float32).astype(ml_dtypes.bfloat16)
    return high, low


@functools.lru_cache(maxsize=None)
def tables(blocks, chans, rows):
    period = 2 * blocks * rows
    s = np.arange(blocks, dtype=np.float64)
    r = np.arange(rows, dtype=np.float64)
    odd = np.arange(blocks, dtype=np.float64) + 0.5
    outer = 2 * np.pi * odd[:, None] * s[None, :] / (2 * blocks)
    eye = np.eye(chans)
    real = np.einsum("ks,cd->cksd", np.cos(outer), eye).reshape(chans * blocks, blocks * chans)
    imag = np.einsum("ks,cd->cksd", -np.sin(outer), eye).reshape(chans * blocks, blocks * chans)
    first = np.concatenate([real, imag], axis=0)
    inner = 2 * np.pi * (np.outer(r, r) % rows) / rows
    cosine, sine = np.cos(inner), np.sin(inner)
    second = np.block([[cosine, -sine], [sine, cosine]])
    twist = 2 * np.pi * odd[:, None] * r[None, :] / period
    return np.concatenate(
        [
            np.concatenate(split_np(np.cos(twist)), axis=1),
            np.concatenate(split_np(np.sin(twist)), axis=1),
            np.concatenate(split_np(first), axis=1),
            *split_np(second),
            *split_np(second.T.copy()),
            *split_np(first.T * (2.0 / period)),
        ],
        axis=0,
    )


class Constants:
    def __init__(self, ref, blocks, rows):
        inner = ref.shape[1]
        start = 0

        def take(count):
            nonlocal start
            start += count
            return slice(start - count, start)

        cosine, sine, first = take(blocks), take(blocks), take(2 * rows)
        high, low = slice(0, rows), slice(rows, 2 * rows)
        self.cosine = lambda: ref[cosine, high].astype(F32) + ref[cosine, low].astype(F32)
        self.sine = lambda: ref[sine, high].astype(F32) + ref[sine, low].astype(F32)
        self.first = (ref.at[first, high], ref.at[first, low])
        self.second = (ref.at[take(inner)], ref.at[take(inner)])
        self.early = start
        self.third = (ref.at[take(inner)], ref.at[take(inner)])
        self.fourth = (ref.at[take(rows)], ref.at[take(rows)])


def split(values):
    high = values.astype(BF)
    return high, (values - high.astype(F32)).astype(BF)


def mm(left, right):
    return jnp.dot(left, right, preferred_element_type=F32)


def twiddle(real, imag, cosine, sine):
    rows, lanes = real.shape
    blocks = cosine.shape[0]
    shape = (rows // blocks, blocks, lanes)
    cosine = cosine[None]
    sine = sine[None]
    real = real.reshape(shape)
    imag = imag.reshape(shape)
    return (
        (real * cosine + imag * sine).reshape(rows, lanes),
        (imag * cosine - real * sine).reshape(rows, lanes),
    )


def forward(values, low_too, constants):
    first_high, first_low = constants.first
    second_high, second_low = constants.second
    high, low = split(values)
    stage = mm(first_high[...], high) + mm(first_low[...], high)
    if low_too:
        stage = stage + mm(first_high[...], low)
    half = stage.shape[0] // 2
    real, imag = twiddle(stage[:half], stage[half:], constants.cosine(), constants.sine())
    high, low = split(jnp.concatenate([real, imag], axis=1))
    return mm(high, second_high[...]) + mm(low, second_high[...]) + mm(high, second_low[...])


def inverse(real, imag, constants):
    third_high, third_low = constants.third
    fourth_high, fourth_low = constants.fourth
    high, low = split(jnp.concatenate([real, imag], axis=1))
    stage = mm(high, third_high[...]) + mm(low, third_high[...]) + mm(high, third_low[...])
    half = stage.shape[1] // 2
    real, imag = twiddle(stage[:, :half], stage[:, half:], constants.cosine(), -constants.sine())
    high, low = split(jnp.concatenate([real, imag], axis=0))
    return mm(fourth_high[...], high) + mm(fourth_high[...], low) + mm(fourth_low[...], high)


def spread(values, wide_ref):
    wide_ref[...] = values.reshape(wide_ref.shape)


def group_of(wide_ref, group):
    blocks, _, size, lanes = wide_ref.shape
    return wide_ref[:, group].reshape(blocks * size, lanes)


def joined(wide_ref):
    blocks, groups, size, lanes = wide_ref.shape
    return wide_ref[...].reshape(blocks * groups * size, lanes)


def started(copies):
    for copy in copies:
        copy.start()
    return copies


def onehots(ids_ref, s, chans, vocab):
    quarter = chans // 4
    lanes = ids_ref.shape[1]
    block = ids_ref[pl.ds(pl.multiple_of(s * chans, chans), chans), :]
    block = block.astype(F32)
    labels = lax.broadcasted_iota(jnp.int32, (16, lanes), 0).astype(F32)
    halves = []
    for half in range(2):
        coarse = jnp.broadcast_to(block[half * quarter : half * quarter + 1], (16, lanes))
        fine = block[(2 + half) * quarter : (2 + half) * quarter + 1]
        fine_hot = (labels == fine).astype(F32).astype(BF)
        coarse = coarse.astype(BF)
        zero = jnp.zeros_like(fine_hot)
        halves.append(
            jnp.concatenate(
                [
                    jnp.where(coarse == jnp.array(part, BF), fine_hot, zero)
                    for part in range(vocab // 16)
                ],
                axis=0,
            )
        )
    return jnp.concatenate(halves, axis=1)


def send_kernel(f_ref, ids_ref, out_ref):
    rows, width = f_ref.shape
    out_ref[:, :rows] = f_ref[...].T.astype(BF)
    ids = ids_ref[...]
    coarse = ids // 16
    pieces = (coarse, ids - 16 * coarse)
    lanes = 128
    quarters = [
        jnp.broadcast_to(piece[:, half * lanes : (half + 1) * lanes].astype(F32), (4, lanes))
        for piece in pieces
        for half in range(2)
    ]
    tile = jnp.concatenate(quarters, axis=0).astype(BF)
    for start in range(0, width, 16):
        out_ref[start : start + 16, rows:] = tile


def front_kernel(
    scale, in_ref, tab_ref, constants_hbm, parts_hbm, spectra_hbm, mixed_ref,
    constants_ref, parts_ref, spectra_ref, wide_ref, in_sems, out_sems,
):
    width, rows = mixed_ref.shape
    chans = tab_ref.shape[0] // 3
    vocab = tab_ref.shape[1]
    blocks = width // chans
    half = width // 2
    size = wide_ref.shape[2]
    constants = Constants(constants_ref, blocks, rows)
    total = constants_ref.shape[0]
    incoming = started(
        [
            pltpu.make_async_copy(constants_hbm.at[part], constants_ref.at[part], in_sems.at[place])
            for place, part in enumerate((slice(0, constants.early), slice(constants.early, total)))
        ]
    )
    query, key, value, ids = (slice(rows * part, rows * (part + 1)) for part in range(4))
    ids = slice(3 * rows, parts_ref.shape[1])
    parts_ref[:, ids] = in_ref[:, rows:]

    def body(s, carry):
        picked = mm(tab_ref[...], onehots(in_ref.at[:, rows:], s, chans, vocab)).astype(BF)
        place = pl.ds(pl.multiple_of(s * chans, chans), chans)
        parts_ref[place, query] = picked[:chans]
        parts_ref[place, key] = picked[chans : 2 * chans]
        parts_ref[place, value] = picked[2 * chans :]
        return carry

    lax.fori_loop(0, blocks, body, 0, unroll=8)
    leaving = started([pltpu.make_async_copy(parts_ref, parts_hbm, out_sems.at[0])])
    incoming[0].wait()
    spread(in_ref[:, :rows].astype(F32), wide_ref)
    fr, fi, gr, gi, cause = (slice(rows * part, rows * (part + 1)) for part in range(5))
    for group in range(2):
        place = slice(group * half, (group + 1) * half)
        spectra_ref[place, : 2 * rows] = forward(group_of(wide_ref, group), False, constants) * scale
    spread(parts_ref[:, key].astype(F32) * parts_ref[:, value].astype(F32), wide_ref)
    for group in range(2):
        place = slice(group * half, (group + 1) * half)
        spectra_ref[place, 2 * rows : 4 * rows] = forward(
            group_of(wide_ref, group), True, constants
        )
    leaving += started(
        [
            pltpu.make_async_copy(
                spectra_ref.at[:, : 4 * rows], spectra_hbm.at[:, : 4 * rows], out_sems.at[1]
            )
        ]
    )
    incoming[1].wait()
    for group in range(2):
        place = slice(group * half, (group + 1) * half)
        a, b = spectra_ref[place, fr], spectra_ref[place, fi]
        c, d = spectra_ref[place, gr], spectra_ref[place, gi]
        causal = inverse(c * a - d * b, c * b + d * a, constants)
        wide_ref[:, group] = causal.reshape(blocks, size, rows)
    causal = joined(wide_ref)
    spectra_ref[:, cause] = causal
    leaving += started(
        [
            pltpu.make_async_copy(
                spectra_ref.at[:, cause], spectra_hbm.at[:, cause], out_sems.at[2]
            )
        ]
    )
    mixed_ref[...] = (parts_ref[:, query].astype(F32) * causal).astype(BF)
    for copy in leaving:
        copy.wait()


def back_kernel(
    scale, b_ref, constants_ref, parts_ref, spectra_ref, out_ref,
    act_ref, spec_ref, acc_ref, wide_ref,
):
    width, rows = b_ref.shape
    blocks = act_ref.shape[0]
    chans = width // blocks
    vocab = acc_ref.shape[0]
    half = width // 2
    size = wide_ref.shape[2]
    shape = (blocks, chans, rows)
    constants = Constants(constants_ref, blocks, rows)
    query, key, value = (slice(rows * part, rows * (part + 1)) for part in range(3))
    ids = slice(3 * rows, parts_ref.shape[1])
    spread(b_ref[...].astype(F32) * parts_ref[:, query].astype(F32), wide_ref)
    for group in range(2):
        place = slice(group * half, (group + 1) * half)
        spec_ref[place] = forward(group_of(wide_ref, group), True, constants)

    def correlate(start):
        for group in range(2):
            place = slice(group * half, (group + 1) * half)
            cr, ci = spec_ref[place, :rows], spec_ref[place, rows:]
            xr = spectra_ref[place, start : start + rows]
            xi = spectra_ref[place, start + rows : start + 2 * rows]
            result = inverse(xr * cr + xi * ci, xr * ci - xi * cr, constants)
            wide_ref[:, group] = result.reshape(blocks, size, rows)
        return joined(wide_ref)

    out_ref[:, :rows] = (correlate(2 * rows) * scale).astype(BF)
    causal = spectra_ref[:, 4 * rows :]
    act_ref[:, :chans] = (b_ref[...].astype(F32) * causal).astype(BF).reshape(shape)
    gated_grad = correlate(0)
    act_ref[:, chans : 2 * chans] = (
        (gated_grad * parts_ref[:, value].astype(F32)).astype(BF).reshape(shape)
    )
    act_ref[:, 2 * chans :] = (
        (gated_grad * parts_ref[:, key].astype(F32)).astype(BF).reshape(shape)
    )
    acc_ref[...] = jnp.zeros_like(acc_ref)
    group = 4

    def body(step, carry):
        hot = jnp.concatenate(
            [onehots(parts_ref.at[:, ids], step * group + g, chans, vocab) for g in range(group)],
            axis=1,
        )
        act = jnp.concatenate([act_ref[step * group + g] for g in range(group)], axis=1)
        acc_ref[:, : 3 * chans] += lax.dot_general(
            hot, act, (((1,), (1,)), ((), ())), preferred_element_type=F32
        )
        return carry

    lax.fori_loop(0, blocks // group, body, 0, unroll=blocks // group)
    out_ref[:, rows:] = acc_ref[...].astype(BF)


def output_kernel(mixed_ref, w_hbm, out_hbm, w_ref, out_ref, in_sems, out_sems):
    chunks, _, lanes = out_ref.shape
    pieces = in_sems.shape[0]
    many = chunks // pieces
    parts = [slice(part * many * lanes, (part + 1) * many * lanes) for part in range(pieces)]
    incoming = started(
        [
            pltpu.make_async_copy(w_hbm.at[:, part], w_ref.at[:, part], in_sems.at[place])
            for place, part in enumerate(parts)
        ]
    )
    left = mixed_ref[...].astype(F32).T.astype(BF)
    leaving = []
    for chunk in range(chunks):
        if chunk % many == 0:
            incoming[chunk // many].wait()
        out_ref[chunk] = mm(left, w_ref[:, chunk * lanes : (chunk + 1) * lanes]).astype(BF)
        leaving += started(
            [pltpu.make_async_copy(out_ref.at[chunk], out_hbm.at[chunk], out_sems.at[chunk])]
        )
    for copy in leaving:
        copy.wait()


def finish_kernel(in_ref, grad_ref, table_ref):
    width, rows = grad_ref.shape[1], grad_ref.shape[0]
    vocab_rows = table_ref.shape[1]
    chans = vocab_rows * width // in_ref.shape[0]
    grad_ref[...] = in_ref[:, :rows].astype(F32).T
    sums = in_ref[:, rows:]
    lanes = sums.shape[1]
    column = lax.broadcasted_iota(jnp.int32, (lanes, width), 1)
    row = lax.broadcasted_iota(jnp.int32, (lanes, width), 0)
    source = lax.broadcasted_iota(jnp.int32, (width, width), 0) // vocab_rows
    mine = source == lax.broadcasted_iota(jnp.int32, (width, width), 1) // chans
    pick = lax.broadcasted_iota(jnp.int32, (vocab_rows, width), 1) % vocab_rows
    pick = pick == lax.broadcasted_iota(jnp.int32, (vocab_rows, width), 0)
    pick = pick.astype(F32).astype(BF)
    for field in range(3):
        take = (row == field * chans + column % chans).astype(F32).astype(BF)
        spreaded = jnp.where(mine, mm(sums, take), 0.0).astype(BF)
        table_ref[field] = mm(pick, spreaded)


def params(mebibytes):
    return pltpu.CompilerParams(vmem_limit_bytes=mebibytes * 1024 * 1024)


HBM = pl.BlockSpec(memory_space=pltpu.HBM)
VMEM = pl.BlockSpec(memory_space=pltpu.VMEM)
DMA = pltpu.SemaphoreType.DMA


def shards(token_ids, table, filter_raw, w_out, cotangent):
    rows = token_ids.shape[0]
    blocks = lax.axis_size("ctx")
    width, features = w_out.shape
    chans = width // blocks
    vocab = table.shape[0]
    length = rows * blocks
    position = lax.axis_index("ctx")
    scale = 1.0 / math.sqrt(length)
    constants = tables(blocks, chans // 2, rows)
    struct = jax.ShapeDtypeStruct
    field = struct((width, rows), BF)
    parts = struct((width, 3 * rows + 128), BF)
    spectra = struct((width, 5 * rows), F32)
    parcel = struct((width, rows + 128), BF)
    spread_shape = pltpu.VMEM((blocks, 2, chans // 2, rows), F32)

    def exchange(values):
        return lax.all_to_all(values, "ctx", split_axis=0, concat_axis=0, tiled=True)

    sent = pl.pallas_call(
        send_kernel, out_shape=parcel, compiler_params=params(62), name="send"
    )(filter_raw, token_ids[None])
    received = exchange(sent)
    cot_full = lax.all_gather(cotangent, "tp", axis=1, tiled=True)

    local = lax.dynamic_slice(table, (0, 0, position * chans), (vocab, 3, chans))
    local = local.transpose(1, 2, 0).reshape(3 * chans, vocab)
    held, spectra_held, mixed = pl.pallas_call(
        functools.partial(front_kernel, scale),
        out_shape=(parts, spectra, field),
        in_specs=[VMEM, VMEM, HBM],
        out_specs=(HBM, HBM, VMEM),
        scratch_shapes=[
            pltpu.VMEM(constants.shape, BF),
            pltpu.VMEM(parts.shape, BF),
            pltpu.VMEM(spectra.shape, F32),
            spread_shape,
            DMA((2,)),
            DMA((3,)),
        ],
        compiler_params=params(50),
        name="front",
    )(received, local, constants)
    mixed_rows = exchange(mixed)
    blocked = struct((features // width, rows, width), BF)
    partial_out = pl.pallas_call(
        output_kernel,
        out_shape=blocked,
        in_specs=[VMEM, HBM],
        out_specs=HBM,
        scratch_shapes=[
            pltpu.VMEM(w_out.shape, BF),
            pltpu.VMEM(blocked.shape, BF),
            DMA((4,)),
            DMA((blocked.shape[0],)),
        ],
        compiler_params=params(61),
        name="project_out",
    )(mixed_rows, w_out)
    output = lax.psum_scatter(
        partial_out.reshape(-1, width), "tp", scatter_dimension=0, tiled=True
    )

    back = lax.dot_general(
        w_out, cot_full, (((1,), (1,)), ((), ())), preferred_element_type=F32
    ).astype(BF)
    back_field = exchange(back)
    grads = pl.pallas_call(
        functools.partial(back_kernel, scale),
        out_shape=parcel,
        scratch_shapes=[
            pltpu.VMEM((blocks, 3 * chans, rows), BF),
            pltpu.VMEM((width, 2 * rows), F32),
            pltpu.VMEM((vocab, 128), F32),
            spread_shape,
        ],
        compiler_params=params(24),
        name="back",
    )(back_field, constants, held, spectra_held)
    grads = exchange(grads)
    vocab_rows = vocab // blocks
    grad_filter, grad_table = pl.pallas_call(
        finish_kernel,
        out_shape=(struct((rows, width), F32), struct((3, vocab_rows, width), F32)),
        compiler_params=params(8),
        name="finish",
    )(grads)
    return (output, grad_filter, grad_table.transpose(1, 0, 2))


def solution(mesh):
    return jax.shard_map(
        shards,
        mesh=mesh,
        in_specs=(P("ctx"), P(None, None, "tp"), P("ctx", "tp"), P("tp", None), P("ctx", "tp")),
        out_specs=(P("ctx", "tp"), P("ctx", "tp"), P("ctx", None, "tp")),
        check_vma=False,
    )
```

```python
import functools
import math

import jax
import jax.numpy as jnp
import ml_dtypes
import numpy as np
from jax import lax
from jax.experimental import pallas as pl
from jax.experimental.pallas import tpu as pltpu
from jax.sharding import PartitionSpec as P

BF = jnp.bfloat16
F32 = jnp.float32


def split_np(values):
    high = values.astype(np.float32).astype(ml_dtypes.bfloat16)
    low = (values - high.astype(np.float64)).astype(np.float32).astype(ml_dtypes.bfloat16)
    return high, low


@functools.lru_cache(maxsize=None)
def tables(blocks, chans, rows):
    period = 2 * blocks * rows
    s = np.arange(blocks, dtype=np.float64)
    r = np.arange(rows, dtype=np.float64)
    odd = np.arange(blocks, dtype=np.float64) + 0.5
    outer = 2 * np.pi * odd[:, None] * s[None, :] / (2 * blocks)
    eye = np.eye(chans)
    real = np.einsum("ks,cd->cksd", np.cos(outer), eye).reshape(chans * blocks, blocks * chans)
    imag = np.einsum("ks,cd->cksd", -np.sin(outer), eye).reshape(chans * blocks, blocks * chans)
    first = np.concatenate([real, imag], axis=0)
    inner = 2 * np.pi * (np.outer(r, r) % rows) / rows
    cosine, sine = np.cos(inner), np.sin(inner)
    second = np.block([[cosine, -sine], [sine, cosine]])
    twist = 2 * np.pi * odd[:, None] * r[None, :] / period
    return np.concatenate(
        [
            np.concatenate(split_np(np.cos(twist)), axis=1),
            np.concatenate(split_np(np.sin(twist)), axis=1),
            np.concatenate(split_np(first), axis=1),
            *split_np(second),
            *split_np(second.T.copy()),
            *split_np(first.T * (2.0 / period)),
        ],
        axis=0,
    )


class Constants:
    def __init__(self, ref, blocks, rows):
        inner = ref.shape[1]
        start = 0

        def take(count):
            nonlocal start
            start += count
            return slice(start - count, start)

        cosine, sine, first = take(blocks), take(blocks), take(2 * rows)
        high, low = slice(0, rows), slice(rows, 2 * rows)
        self.cosine = lambda: ref[cosine, high].astype(F32) + ref[cosine, low].astype(F32)
        self.sine = lambda: ref[sine, high].astype(F32) + ref[sine, low].astype(F32)
        self.first = (ref.at[first, high], ref.at[first, low])
        self.second = (ref.at[take(inner)], ref.at[take(inner)])
        self.early = start
        self.third = (ref.at[take(inner)], ref.at[take(inner)])
        self.fourth = (ref.at[take(rows)], ref.at[take(rows)])


def split(values):
    high = values.astype(BF)
    return high, (values - high.astype(F32)).astype(BF)


def mm(left, right):
    return jnp.dot(left, right, preferred_element_type=F32)


def twiddle(real, imag, cosine, sine):
    rows, lanes = real.shape
    blocks = cosine.shape[0]
    shape = (rows // blocks, blocks, lanes)
    cosine = cosine[None]
    sine = sine[None]
    real = real.reshape(shape)
    imag = imag.reshape(shape)
    return (
        (real * cosine + imag * sine).reshape(rows, lanes),
        (imag * cosine - real * sine).reshape(rows, lanes),
    )


def forward(values, low_too, constants):
    first_high, first_low = constants.first
    second_high, second_low = constants.second
    high, low = split(values)
    stage = mm(first_high[...], high) + mm(first_low[...], high)
    if low_too:
        stage = stage + mm(first_high[...], low)
    half = stage.shape[0] // 2
    real, imag = twiddle(stage[:half], stage[half:], constants.cosine(), constants.sine())
    high, low = split(jnp.concatenate([real, imag], axis=1))
    return mm(high, second_high[...]) + mm(low, second_high[...]) + mm(high, second_low[...])


def inverse(real, imag, constants):
    third_high, third_low = constants.third
    fourth_high, fourth_low = constants.fourth
    high, low = split(jnp.concatenate([real, imag], axis=1))
    stage = mm(high, third_high[...]) + mm(low, third_high[...]) + mm(high, third_low[...])
    half = stage.shape[1] // 2
    real, imag = twiddle(stage[:, :half], stage[:, half:], constants.cosine(), -constants.sine())
    high, low = split(jnp.concatenate([real, imag], axis=0))
    return mm(fourth_high[...], high) + mm(fourth_high[...], low) + mm(fourth_low[...], high)


def spread(values, wide_ref):
    wide_ref[...] = values.reshape(wide_ref.shape)


def group_of(wide_ref, group):
    blocks, _, size, lanes = wide_ref.shape
    return wide_ref[:, group].reshape(blocks * size, lanes)


def joined(wide_ref):
    blocks, groups, size, lanes = wide_ref.shape
    return wide_ref[...].reshape(blocks * groups * size, lanes)


def started(copies):
    for copy in copies:
        copy.start()
    return copies


def onehots(ids_ref, s, chans, vocab):
    quarter = chans // 4
    lanes = ids_ref.shape[1]
    block = ids_ref[pl.ds(pl.multiple_of(s * chans, chans), chans), :]
    block = block.astype(F32)
    labels = lax.broadcasted_iota(jnp.int32, (16, lanes), 0).astype(F32)
    halves = []
    for half in range(2):
        coarse = jnp.broadcast_to(block[half * quarter : half * quarter + 1], (16, lanes))
        fine = block[(2 + half) * quarter : (2 + half) * quarter + 1]
        fine_hot = (labels == fine).astype(F32).astype(BF)
        coarse = coarse.astype(BF)
        zero = jnp.zeros_like(fine_hot)
        halves.append(
            jnp.concatenate(
                [
                    jnp.where(coarse == jnp.array(part, BF), fine_hot, zero)
                    for part in range(vocab // 16)
                ],
                axis=0,
            )
        )
    return jnp.concatenate(halves, axis=1)


def send_kernel(f_ref, ids_ref, out_ref):
    rows, width = f_ref.shape
    out_ref[:, :rows] = f_ref[...].T.astype(BF)
    ids = ids_ref[...]
    coarse = ids // 16
    pieces = (coarse, ids - 16 * coarse)
    lanes = 128
    quarters = [
        jnp.broadcast_to(piece[:, half * lanes : (half + 1) * lanes].astype(F32), (4, lanes))
        for piece in pieces
        for half in range(2)
    ]
    tile = jnp.concatenate(quarters, axis=0).astype(BF)
    for start in range(0, width, 16):
        out_ref[start : start + 16, rows:] = tile


def front_kernel(
    scale, in_ref, tab_ref, constants_hbm, parts_hbm, spectra_hbm, mixed_ref,
    constants_ref, parts_ref, spectra_ref, wide_ref, in_sems, out_sems,
):
    width, rows = mixed_ref.shape
    chans = tab_ref.shape[0] // 3
    vocab = tab_ref.shape[1]
    blocks = width // chans
    half = width // 2
    size = wide_ref.shape[2]
    constants = Constants(constants_ref, blocks, rows)
    total = constants_ref.shape[0]
    incoming = started(
        [
            pltpu.make_async_copy(constants_hbm.at[part], constants_ref.at[part], in_sems.at[place])
            for place, part in enumerate((slice(0, constants.early), slice(constants.early, total)))
        ]
    )
    query, key, value, ids = (slice(rows * part, rows * (part + 1)) for part in range(4))
    ids = slice(3 * rows, parts_ref.shape[1])
    parts_ref[:, ids] = in_ref[:, rows:]

    def body(s, carry):
        picked = mm(tab_ref[...], onehots(in_ref.at[:, rows:], s, chans, vocab)).astype(BF)
        place = pl.ds(pl.multiple_of(s * chans, chans), chans)
        parts_ref[place, query] = picked[:chans]
        parts_ref[place, key] = picked[chans : 2 * chans]
        parts_ref[place, value] = picked[2 * chans :]
        return carry

    lax.fori_loop(0, blocks, body, 0, unroll=blocks)
    leaving = started([pltpu.make_async_copy(parts_ref, parts_hbm, out_sems.at[0])])
    incoming[0].wait()
    spread(in_ref[:, :rows].astype(F32), wide_ref)
    fr, fi, gr, gi, cause = (slice(rows * part, rows * (part + 1)) for part in range(5))
    for group in range(2):
        place = slice(group * half, (group + 1) * half)
        spectra_ref[place, : 2 * rows] = forward(group_of(wide_ref, group), False, constants) * scale
    spread(parts_ref[:, key].astype(F32) * parts_ref[:, value].astype(F32), wide_ref)
    for group in range(2):
        place = slice(group * half, (group + 1) * half)
        spectra_ref[place, 2 * rows : 4 * rows] = forward(
            group_of(wide_ref, group), True, constants
        )
    leaving += started(
        [
            pltpu.make_async_copy(
                spectra_ref.at[:, : 4 * rows], spectra_hbm.at[:, : 4 * rows], out_sems.at[1]
            )
        ]
    )
    incoming[1].wait()
    for group in range(2):
        place = slice(group * half, (group + 1) * half)
        a, b = spectra_ref[place, fr], spectra_ref[place, fi]
        c, d = spectra_ref[place, gr], spectra_ref[place, gi]
        causal = inverse(c * a - d * b, c * b + d * a, constants)
        wide_ref[:, group] = causal.reshape(blocks, size, rows)
    causal = joined(wide_ref)
    spectra_ref[:, cause] = causal
    leaving += started(
        [
            pltpu.make_async_copy(
                spectra_ref.at[:, cause], spectra_hbm.at[:, cause], out_sems.at[2]
            )
        ]
    )
    mixed_ref[...] = (parts_ref[:, query].astype(F32) * causal).astype(BF)
    for copy in leaving:
        copy.wait()


def back_kernel(
    scale, b_ref, constants_ref, parts_ref, spectra_ref, out_ref,
    act_ref, spec_ref, acc_ref, wide_ref,
):
    width, rows = b_ref.shape
    blocks = act_ref.shape[0]
    chans = width // blocks
    vocab = acc_ref.shape[0]
    half = width // 2
    size = wide_ref.shape[2]
    shape = (blocks, chans, rows)
    constants = Constants(constants_ref, blocks, rows)
    query, key, value = (slice(rows * part, rows * (part + 1)) for part in range(3))
    ids = slice(3 * rows, parts_ref.shape[1])
    spread(b_ref[...].astype(F32) * parts_ref[:, query].astype(F32), wide_ref)
    for group in range(2):
        place = slice(group * half, (group + 1) * half)
        spec_ref[place] = forward(group_of(wide_ref, group), True, constants)

    def correlate(start):
        for group in range(2):
            place = slice(group * half, (group + 1) * half)
            cr, ci = spec_ref[place, :rows], spec_ref[place, rows:]
            xr = spectra_ref[place, start : start + rows]
            xi = spectra_ref[place, start + rows : start + 2 * rows]
            result = inverse(xr * cr + xi * ci, xr * ci - xi * cr, constants)
            wide_ref[:, group] = result.reshape(blocks, size, rows)
        return joined(wide_ref)

    out_ref[:, :rows] = (correlate(2 * rows) * scale).astype(BF)
    causal = spectra_ref[:, 4 * rows :]
    act_ref[:, :chans] = (b_ref[...].astype(F32) * causal).astype(BF).reshape(shape)
    gated_grad = correlate(0)
    act_ref[:, chans : 2 * chans] = (
        (gated_grad * parts_ref[:, value].astype(F32)).astype(BF).reshape(shape)
    )
    act_ref[:, 2 * chans :] = (
        (gated_grad * parts_ref[:, key].astype(F32)).astype(BF).reshape(shape)
    )
    acc_ref[...] = jnp.zeros_like(acc_ref)
    group = 4

    def body(step, carry):
        hot = jnp.concatenate(
            [onehots(parts_ref.at[:, ids], step * group + g, chans, vocab) for g in range(group)],
            axis=1,
        )
        act = jnp.concatenate([act_ref[step * group + g] for g in range(group)], axis=1)
        acc_ref[:, : 3 * chans] += lax.dot_general(
            hot, act, (((1,), (1,)), ((), ())), preferred_element_type=F32
        )
        return carry

    lax.fori_loop(0, blocks // group, body, 0, unroll=blocks // group)
    out_ref[:, rows:] = acc_ref[...].astype(BF)


def finish_kernel(in_ref, grad_ref, table_ref):
    width, rows = grad_ref.shape[1], grad_ref.shape[0]
    vocab_rows = table_ref.shape[1]
    chans = vocab_rows * width // in_ref.shape[0]
    grad_ref[...] = in_ref[:, :rows].astype(F32).T
    sums = in_ref[:, rows:]
    lanes = sums.shape[1]
    column = lax.broadcasted_iota(jnp.int32, (lanes, width), 1)
    row = lax.broadcasted_iota(jnp.int32, (lanes, width), 0)
    source = lax.broadcasted_iota(jnp.int32, (width, width), 0) // vocab_rows
    mine = source == lax.broadcasted_iota(jnp.int32, (width, width), 1) // chans
    pick = lax.broadcasted_iota(jnp.int32, (vocab_rows, width), 1) % vocab_rows
    pick = pick == lax.broadcasted_iota(jnp.int32, (vocab_rows, width), 0)
    pick = pick.astype(F32).astype(BF)
    for field in range(3):
        take = (row == field * chans + column % chans).astype(F32).astype(BF)
        spreaded = jnp.where(mine, mm(sums, take), 0.0).astype(BF)
        table_ref[field] = mm(pick, spreaded)


def params(mebibytes):
    return pltpu.CompilerParams(vmem_limit_bytes=mebibytes * 1024 * 1024)


HBM = pl.BlockSpec(memory_space=pltpu.HBM)
VMEM = pl.BlockSpec(memory_space=pltpu.VMEM)
DMA = pltpu.SemaphoreType.DMA


def shards(token_ids, table, filter_raw, w_out, cotangent):
    rows = token_ids.shape[0]
    blocks = lax.axis_size("ctx")
    width, features = w_out.shape
    chans = width // blocks
    vocab = table.shape[0]
    length = rows * blocks
    position = lax.axis_index("ctx")
    scale = 1.0 / math.sqrt(length)
    constants = tables(blocks, chans // 2, rows)
    struct = jax.ShapeDtypeStruct
    field = struct((width, rows), BF)
    parts = struct((width, 3 * rows + 128), BF)
    spectra = struct((width, 5 * rows), F32)
    parcel = struct((width, rows + 128), BF)
    spread_shape = pltpu.VMEM((blocks, 2, chans // 2, rows), F32)
    chunks = 8
    lanes = features // chunks

    def exchange(values):
        return lax.all_to_all(values, "ctx", split_axis=0, concat_axis=0, tiled=True)

    sent = pl.pallas_call(
        send_kernel, out_shape=parcel, compiler_params=params(62), name="send"
    )(filter_raw, token_ids[None])
    local = lax.dynamic_slice(table, (0, 0, position * chans), (vocab, 3, chans))
    local = local.transpose(1, 2, 0).reshape(3 * chans, vocab)
    sent, local = lax.optimization_barrier((sent, local))
    received = exchange(sent)
    cot_full = lax.all_gather(cotangent, "tp", axis=1, tiled=True)

    held, spectra_held, mixed = pl.pallas_call(
        functools.partial(front_kernel, scale),
        out_shape=(parts, spectra, field),
        in_specs=[VMEM, VMEM, HBM],
        out_specs=(HBM, HBM, VMEM),
        scratch_shapes=[
            pltpu.VMEM(constants.shape, BF),
            pltpu.VMEM(parts.shape, BF),
            pltpu.VMEM(spectra.shape, F32),
            spread_shape,
            DMA((2,)),
            DMA((3,)),
        ],
        compiler_params=params(50),
        name="front",
    )(received, local, constants)
    mixed_rows = exchange(mixed)
    partial_out = lax.dot_general(
        mixed_rows, w_out, (((0,), (0,)), ((), ())), preferred_element_type=F32
    ).astype(BF)
    output = lax.psum_scatter(partial_out, "tp", scatter_dimension=1, tiled=True)

    back = lax.dot_general(
        w_out, cot_full, (((1,), (1,)), ((), ())), preferred_element_type=F32
    ).astype(BF)
    back_field = exchange(back)
    grads = pl.pallas_call(
        functools.partial(back_kernel, scale),
        out_shape=parcel,
        scratch_shapes=[
            pltpu.VMEM((blocks, 3 * chans, rows), BF),
            pltpu.VMEM((width, 2 * rows), F32),
            pltpu.VMEM((vocab, 128), F32),
            spread_shape,
        ],
        compiler_params=params(24),
        name="back",
    )(back_field, constants, held, spectra_held)
    grads = exchange(grads)
    vocab_rows = vocab // blocks
    grad_filter, grad_table = pl.pallas_call(
        finish_kernel,
        out_shape=(struct((rows, width), F32), struct((3, vocab_rows, width), F32)),
        compiler_params=params(8),
        name="finish",
    )(grads)
    return (output, grad_filter, grad_table.transpose(1, 0, 2))


def solution(mesh):
    return jax.shard_map(
        shards,
        mesh=mesh,
        in_specs=(P("ctx"), P(None, None, "tp"), P("ctx", "tp"), P("tp", None), P("ctx", "tp")),
        out_specs=(P("ctx", "tp"), P("ctx", "tp"), P("ctx", None, "tp")),
        check_vma=False,
    )
```

```python
import functools
import math

import jax
import jax.numpy as jnp
import ml_dtypes
import numpy as np
from jax import lax
from jax.experimental import pallas as pl
from jax.experimental.pallas import tpu as pltpu
from jax.sharding import PartitionSpec as P

BF = jnp.bfloat16
F32 = jnp.float32


def split_np(values):
    high = values.astype(np.float32).astype(ml_dtypes.bfloat16)
    low = (values - high.astype(np.float64)).astype(np.float32).astype(ml_dtypes.bfloat16)
    return high, low


@functools.lru_cache(maxsize=None)
def tables(blocks, chans, rows):
    period = 2 * blocks * rows
    s = np.arange(blocks, dtype=np.float64)
    r = np.arange(rows, dtype=np.float64)
    odd = np.arange(blocks, dtype=np.float64) + 0.5
    outer = 2 * np.pi * odd[:, None] * s[None, :] / (2 * blocks)
    eye = np.eye(chans)
    real = np.einsum("ks,cd->cksd", np.cos(outer), eye).reshape(chans * blocks, blocks * chans)
    imag = np.einsum("ks,cd->cksd", -np.sin(outer), eye).reshape(chans * blocks, blocks * chans)
    first = np.concatenate([real, imag], axis=0)
    inner = 2 * np.pi * (np.outer(r, r) % rows) / rows
    cosine, sine = np.cos(inner), np.sin(inner)
    second = np.block([[cosine, -sine], [sine, cosine]])
    twist = 2 * np.pi * odd[:, None] * r[None, :] / period
    return np.concatenate(
        [
            np.concatenate(split_np(np.cos(twist)), axis=1),
            np.concatenate(split_np(np.sin(twist)), axis=1),
            np.concatenate(split_np(first), axis=1),
            *split_np(second),
            *split_np(second.T.copy()),
            *split_np(first.T * (2.0 / period)),
        ],
        axis=0,
    )


class Constants:
    def __init__(self, ref, blocks, rows):
        inner = ref.shape[1]
        start = 0

        def take(count):
            nonlocal start
            start += count
            return slice(start - count, start)

        cosine, sine, first = take(blocks), take(blocks), take(2 * rows)
        high, low = slice(0, rows), slice(rows, 2 * rows)
        self.cosine = lambda: ref[cosine, high].astype(F32) + ref[cosine, low].astype(F32)
        self.sine = lambda: ref[sine, high].astype(F32) + ref[sine, low].astype(F32)
        self.first = (ref.at[first, high], ref.at[first, low])
        self.second = (ref.at[take(inner)], ref.at[take(inner)])
        self.early = start
        self.third = (ref.at[take(inner)], ref.at[take(inner)])
        self.fourth = (ref.at[take(rows)], ref.at[take(rows)])


def split(values):
    high = values.astype(BF)
    return high, (values - high.astype(F32)).astype(BF)


def mm(left, right):
    return jnp.dot(left, right, preferred_element_type=F32)


def twiddle(real, imag, cosine, sine):
    rows, lanes = real.shape
    blocks = cosine.shape[0]
    shape = (rows // blocks, blocks, lanes)
    cosine = cosine[None]
    sine = sine[None]
    real = real.reshape(shape)
    imag = imag.reshape(shape)
    return (
        (real * cosine + imag * sine).reshape(rows, lanes),
        (imag * cosine - real * sine).reshape(rows, lanes),
    )


def forward(values, low_too, constants):
    first_high, first_low = constants.first
    second_high, second_low = constants.second
    high, low = split(values)
    stage = mm(first_high[...], high) + mm(first_low[...], high)
    if low_too:
        stage = stage + mm(first_high[...], low)
    half = stage.shape[0] // 2
    real, imag = twiddle(stage[:half], stage[half:], constants.cosine(), constants.sine())
    high, low = split(jnp.concatenate([real, imag], axis=1))
    return mm(high, second_high[...]) + mm(low, second_high[...]) + mm(high, second_low[...])


def inverse(real, imag, constants):
    third_high, third_low = constants.third
    fourth_high, fourth_low = constants.fourth
    high, low = split(jnp.concatenate([real, imag], axis=1))
    stage = mm(high, third_high[...]) + mm(low, third_high[...]) + mm(high, third_low[...])
    half = stage.shape[1] // 2
    real, imag = twiddle(stage[:, :half], stage[:, half:], constants.cosine(), -constants.sine())
    high, low = split(jnp.concatenate([real, imag], axis=0))
    return mm(fourth_high[...], high) + mm(fourth_high[...], low) + mm(fourth_low[...], high)


def spread(values, wide_ref):
    wide_ref[...] = values.reshape(wide_ref.shape)


def group_of(wide_ref, group):
    blocks, _, size, lanes = wide_ref.shape
    return wide_ref[:, group].reshape(blocks * size, lanes)


def joined(wide_ref):
    blocks, groups, size, lanes = wide_ref.shape
    return wide_ref[...].reshape(blocks * groups * size, lanes)


def started(copies):
    for copy in copies:
        copy.start()
    return copies


def onehots(ids_ref, s, chans, vocab):
    quarter = chans // 4
    lanes = ids_ref.shape[1]
    block = ids_ref[pl.ds(pl.multiple_of(s * chans, chans), chans), :]
    block = block.astype(F32)
    labels = lax.broadcasted_iota(jnp.int32, (16, lanes), 0).astype(F32)
    halves = []
    for half in range(2):
        coarse = jnp.broadcast_to(block[half * quarter : half * quarter + 1], (16, lanes))
        fine = block[(2 + half) * quarter : (2 + half) * quarter + 1]
        fine_hot = (labels == fine).astype(F32).astype(BF)
        coarse = coarse.astype(BF)
        zero = jnp.zeros_like(fine_hot)
        halves.append(
            jnp.concatenate(
                [
                    jnp.where(coarse == jnp.array(part, BF), fine_hot, zero)
                    for part in range(vocab // 16)
                ],
                axis=0,
            )
        )
    return jnp.concatenate(halves, axis=1)


def send_kernel(f_ref, ids_ref, out_ref):
    rows, width = f_ref.shape
    out_ref[:, :rows] = f_ref[...].T.astype(BF)
    ids = ids_ref[...]
    coarse = ids // 16
    pieces = (coarse, ids - 16 * coarse)
    lanes = 128
    quarters = [
        jnp.broadcast_to(piece[:, half * lanes : (half + 1) * lanes].astype(F32), (4, lanes))
        for piece in pieces
        for half in range(2)
    ]
    tile = jnp.concatenate(quarters, axis=0).astype(BF)
    for start in range(0, width, 16):
        out_ref[start : start + 16, rows:] = tile


def front_kernel(
    scale, in_ref, tab_ref, constants_hbm, parts_hbm, spectra_hbm, mixed_ref,
    constants_ref, parts_ref, spectra_ref, wide_ref, in_sems, out_sems,
):
    width, rows = mixed_ref.shape
    chans = tab_ref.shape[0] // 3
    vocab = tab_ref.shape[1]
    blocks = width // chans
    half = width // 2
    size = wide_ref.shape[2]
    constants = Constants(constants_ref, blocks, rows)
    total = constants_ref.shape[0]
    incoming = started(
        [
            pltpu.make_async_copy(constants_hbm.at[part], constants_ref.at[part], in_sems.at[place])
            for place, part in enumerate((slice(0, constants.early), slice(constants.early, total)))
        ]
    )
    query, key, value, ids = (slice(rows * part, rows * (part + 1)) for part in range(4))
    ids = slice(3 * rows, parts_ref.shape[1])
    parts_ref[:, ids] = in_ref[:, rows:]

    def body(s, carry):
        picked = mm(tab_ref[...], onehots(in_ref.at[:, rows:], s, chans, vocab)).astype(BF)
        place = pl.ds(pl.multiple_of(s * chans, chans), chans)
        parts_ref[place, query] = picked[:chans]
        parts_ref[place, key] = picked[chans : 2 * chans]
        parts_ref[place, value] = picked[2 * chans :]
        return carry

    lax.fori_loop(0, blocks, body, 0, unroll=8)
    leaving = started([pltpu.make_async_copy(parts_ref, parts_hbm, out_sems.at[0])])
    incoming[0].wait()
    spread(in_ref[:, :rows].astype(F32), wide_ref)
    fr, fi, gr, gi, cause = (slice(rows * part, rows * (part + 1)) for part in range(5))
    for group in range(2):
        place = slice(group * half, (group + 1) * half)
        spectra_ref[place, : 2 * rows] = forward(group_of(wide_ref, group), False, constants) * scale
    spread(parts_ref[:, key].astype(F32) * parts_ref[:, value].astype(F32), wide_ref)
    for group in range(2):
        place = slice(group * half, (group + 1) * half)
        spectra_ref[place, 2 * rows : 4 * rows] = forward(
            group_of(wide_ref, group), True, constants
        )
    leaving += started(
        [
            pltpu.make_async_copy(
                spectra_ref.at[:, : 4 * rows], spectra_hbm.at[:, : 4 * rows], out_sems.at[1]
            )
        ]
    )
    incoming[1].wait()
    for group in range(2):
        place = slice(group * half, (group + 1) * half)
        a, b = spectra_ref[place, fr], spectra_ref[place, fi]
        c, d = spectra_ref[place, gr], spectra_ref[place, gi]
        causal = inverse(c * a - d * b, c * b + d * a, constants)
        wide_ref[:, group] = causal.reshape(blocks, size, rows)
    causal = joined(wide_ref)
    spectra_ref[:, cause] = causal
    leaving += started(
        [
            pltpu.make_async_copy(
                spectra_ref.at[:, cause], spectra_hbm.at[:, cause], out_sems.at[2]
            )
        ]
    )
    mixed_ref[...] = (parts_ref[:, query].astype(F32) * causal).astype(BF)
    for copy in leaving:
        copy.wait()


def back_kernel(
    scale, b_ref, constants_ref, parts_ref, spectra_ref, out_ref,
    act_ref, spec_ref, acc_ref, wide_ref,
):
    width, rows = b_ref.shape
    blocks = act_ref.shape[0]
    chans = width // blocks
    vocab = acc_ref.shape[0]
    half = width // 2
    size = wide_ref.shape[2]
    shape = (blocks, chans, rows)
    constants = Constants(constants_ref, blocks, rows)
    query, key, value = (slice(rows * part, rows * (part + 1)) for part in range(3))
    ids = slice(3 * rows, parts_ref.shape[1])
    spread(b_ref[...].astype(F32) * parts_ref[:, query].astype(F32), wide_ref)
    for group in range(2):
        place = slice(group * half, (group + 1) * half)
        spec_ref[place] = forward(group_of(wide_ref, group), True, constants)

    def correlate(start):
        for group in range(2):
            place = slice(group * half, (group + 1) * half)
            cr, ci = spec_ref[place, :rows], spec_ref[place, rows:]
            xr = spectra_ref[place, start : start + rows]
            xi = spectra_ref[place, start + rows : start + 2 * rows]
            result = inverse(xr * cr + xi * ci, xr * ci - xi * cr, constants)
            wide_ref[:, group] = result.reshape(blocks, size, rows)
        return joined(wide_ref)

    out_ref[:, :rows] = (correlate(2 * rows) * scale).astype(BF)
    causal = spectra_ref[:, 4 * rows :]
    act_ref[:, :chans] = (b_ref[...].astype(F32) * causal).astype(BF).reshape(shape)
    gated_grad = correlate(0)
    act_ref[:, chans : 2 * chans] = (
        (gated_grad * parts_ref[:, value].astype(F32)).astype(BF).reshape(shape)
    )
    act_ref[:, 2 * chans :] = (
        (gated_grad * parts_ref[:, key].astype(F32)).astype(BF).reshape(shape)
    )
    acc_ref[...] = jnp.zeros_like(acc_ref)
    group = 4

    def body(step, carry):
        hot = jnp.concatenate(
            [onehots(parts_ref.at[:, ids], step * group + g, chans, vocab) for g in range(group)],
            axis=1,
        )
        act = jnp.concatenate([act_ref[step * group + g] for g in range(group)], axis=1)
        acc_ref[:, : 3 * chans] += lax.dot_general(
            hot, act, (((1,), (1,)), ((), ())), preferred_element_type=F32
        )
        return carry

    lax.fori_loop(0, blocks // group, body, 0, unroll=blocks // group)
    out_ref[:, rows:] = acc_ref[...].astype(BF)


def finish_kernel(in_ref, grad_ref, table_ref):
    width, rows = grad_ref.shape[1], grad_ref.shape[0]
    vocab_rows = table_ref.shape[1]
    chans = vocab_rows * width // in_ref.shape[0]
    grad_ref[...] = in_ref[:, :rows].astype(F32).T
    sums = in_ref[:, rows:]
    lanes = sums.shape[1]
    column = lax.broadcasted_iota(jnp.int32, (lanes, width), 1)
    row = lax.broadcasted_iota(jnp.int32, (lanes, width), 0)
    source = lax.broadcasted_iota(jnp.int32, (width, width), 0) // vocab_rows
    mine = source == lax.broadcasted_iota(jnp.int32, (width, width), 1) // chans
    pick = lax.broadcasted_iota(jnp.int32, (vocab_rows, width), 1) % vocab_rows
    pick = pick == lax.broadcasted_iota(jnp.int32, (vocab_rows, width), 0)
    pick = pick.astype(F32).astype(BF)
    for field in range(3):
        take = (row == field * chans + column % chans).astype(F32).astype(BF)
        spreaded = jnp.where(mine, mm(sums, take), 0.0).astype(BF)
        table_ref[field] = mm(pick, spreaded)


def params(mebibytes):
    return pltpu.CompilerParams(vmem_limit_bytes=mebibytes * 1024 * 1024)


HBM = pl.BlockSpec(memory_space=pltpu.HBM)
VMEM = pl.BlockSpec(memory_space=pltpu.VMEM)
DMA = pltpu.SemaphoreType.DMA


def shards(token_ids, table, filter_raw, w_out, cotangent):
    rows = token_ids.shape[0]
    blocks = lax.axis_size("ctx")
    width, features = w_out.shape
    chans = width // blocks
    vocab = table.shape[0]
    length = rows * blocks
    position = lax.axis_index("ctx")
    scale = 1.0 / math.sqrt(length)
    constants = tables(blocks, chans // 2, rows)
    struct = jax.ShapeDtypeStruct
    field = struct((width, rows), BF)
    parts = struct((width, 3 * rows + 128), BF)
    spectra = struct((width, 5 * rows), F32)
    parcel = struct((width, rows + 128), BF)
    spread_shape = pltpu.VMEM((blocks, 2, chans // 2, rows), F32)
    chunks = 8
    lanes = features // chunks

    def exchange(values):
        return lax.all_to_all(values, "ctx", split_axis=0, concat_axis=0, tiled=True)

    sent = pl.pallas_call(
        send_kernel, out_shape=parcel, compiler_params=params(62), name="send"
    )(filter_raw, token_ids[None])
    sent, table = lax.optimization_barrier((sent, table))
    local = lax.dynamic_slice(table, (0, 0, position * chans), (vocab, 3, chans))
    local = local.transpose(1, 2, 0).reshape(3 * chans, vocab)
    sent, local = lax.optimization_barrier((sent, local))
    received = exchange(sent)
    cot_full = lax.all_gather(cotangent, "tp", axis=1, tiled=True)

    held, spectra_held, mixed = pl.pallas_call(
        functools.partial(front_kernel, scale),
        out_shape=(parts, spectra, field),
        in_specs=[VMEM, VMEM, HBM],
        out_specs=(HBM, HBM, VMEM),
        scratch_shapes=[
            pltpu.VMEM(constants.shape, BF),
            pltpu.VMEM(parts.shape, BF),
            pltpu.VMEM(spectra.shape, F32),
            spread_shape,
            DMA((2,)),
            DMA((3,)),
        ],
        compiler_params=params(50),
        name="front",
    )(received, local, constants)
    mixed_rows = exchange(mixed)
    partial_out = lax.dot_general(
        mixed_rows, w_out, (((0,), (0,)), ((), ())), preferred_element_type=F32
    ).astype(BF)
    output = lax.psum_scatter(partial_out, "tp", scatter_dimension=1, tiled=True)

    back = lax.dot_general(
        w_out, cot_full, (((1,), (1,)), ((), ())), preferred_element_type=F32
    ).astype(BF)
    back_field = exchange(back)
    grads = pl.pallas_call(
        functools.partial(back_kernel, scale),
        out_shape=parcel,
        scratch_shapes=[
            pltpu.VMEM((blocks, 3 * chans, rows), BF),
            pltpu.VMEM((width, 2 * rows), F32),
            pltpu.VMEM((vocab, 128), F32),
            spread_shape,
        ],
        compiler_params=params(24),
        name="back",
    )(back_field, constants, held, spectra_held)
    grads = exchange(grads)
    vocab_rows = vocab // blocks
    grad_filter, grad_table = pl.pallas_call(
        finish_kernel,
        out_shape=(struct((rows, width), F32), struct((3, vocab_rows, width), F32)),
        compiler_params=params(8),
        name="finish",
    )(grads)
    return (output, grad_filter, grad_table.transpose(1, 0, 2))


def solution(mesh):
    return jax.shard_map(
        shards,
        mesh=mesh,
        in_specs=(P("ctx"), P(None, None, "tp"), P("ctx", "tp"), P("tp", None), P("ctx", "tp")),
        out_specs=(P("ctx", "tp"), P("ctx", "tp"), P("ctx", None, "tp")),
        check_vma=False,
    )
```

```python
import functools
import math

import jax
import jax.numpy as jnp
import ml_dtypes
import numpy as np
from jax import lax
from jax.experimental import pallas as pl
from jax.experimental.pallas import tpu as pltpu
from jax.sharding import PartitionSpec as P

BF = jnp.bfloat16
F32 = jnp.float32


def split_np(values):
    high = values.astype(np.float32).astype(ml_dtypes.bfloat16)
    low = (values - high.astype(np.float64)).astype(np.float32).astype(ml_dtypes.bfloat16)
    return high, low


@functools.lru_cache(maxsize=None)
def tables(blocks, chans, rows):
    period = 2 * blocks * rows
    s = np.arange(blocks, dtype=np.float64)
    r = np.arange(rows, dtype=np.float64)
    odd = np.arange(blocks, dtype=np.float64) + 0.5
    outer = 2 * np.pi * odd[:, None] * s[None, :] / (2 * blocks)
    eye = np.eye(chans)
    real = np.einsum("ks,cd->cksd", np.cos(outer), eye).reshape(chans * blocks, blocks * chans)
    imag = np.einsum("ks,cd->cksd", -np.sin(outer), eye).reshape(chans * blocks, blocks * chans)
    first = np.concatenate([real, imag], axis=0)
    inner = 2 * np.pi * (np.outer(r, r) % rows) / rows
    cosine, sine = np.cos(inner), np.sin(inner)
    second = np.block([[cosine, -sine], [sine, cosine]])
    twist = 2 * np.pi * odd[:, None] * r[None, :] / period
    return np.concatenate(
        [
            np.concatenate(split_np(np.cos(twist)), axis=1),
            np.concatenate(split_np(np.sin(twist)), axis=1),
            np.concatenate(split_np(first), axis=1),
            *split_np(second),
            *split_np(second.T.copy()),
            *split_np(first.T * (2.0 / period)),
        ],
        axis=0,
    )


class Constants:
    def __init__(self, ref, blocks, rows):
        inner = ref.shape[1]
        start = 0

        def take(count):
            nonlocal start
            start += count
            return slice(start - count, start)

        cosine, sine, first = take(blocks), take(blocks), take(2 * rows)
        high, low = slice(0, rows), slice(rows, 2 * rows)
        self.cosine = lambda: ref[cosine, high].astype(F32) + ref[cosine, low].astype(F32)
        self.sine = lambda: ref[sine, high].astype(F32) + ref[sine, low].astype(F32)
        self.first = (ref.at[first, high], ref.at[first, low])
        self.second = (ref.at[take(inner)], ref.at[take(inner)])
        self.early = start
        self.third = (ref.at[take(inner)], ref.at[take(inner)])
        self.fourth = (ref.at[take(rows)], ref.at[take(rows)])


def split(values):
    high = values.astype(BF)
    return high, (values - high.astype(F32)).astype(BF)


def mm(left, right):
    return jnp.dot(left, right, preferred_element_type=F32)


def twiddle(real, imag, cosine, sine):
    rows, lanes = real.shape
    blocks = cosine.shape[0]
    shape = (rows // blocks, blocks, lanes)
    cosine = cosine[None]
    sine = sine[None]
    real = real.reshape(shape)
    imag = imag.reshape(shape)
    return (
        (real * cosine + imag * sine).reshape(rows, lanes),
        (imag * cosine - real * sine).reshape(rows, lanes),
    )


def forward(values, low_too, constants):
    first_high, first_low = constants.first
    second_high, second_low = constants.second
    high, low = split(values)
    stage = mm(first_high[...], high) + mm(first_low[...], high)
    if low_too:
        stage = stage + mm(first_high[...], low)
    half = stage.shape[0] // 2
    real, imag = twiddle(stage[:half], stage[half:], constants.cosine(), constants.sine())
    high, low = split(jnp.concatenate([real, imag], axis=1))
    return mm(high, second_high[...]) + mm(low, second_high[...]) + mm(high, second_low[...])


def inverse(real, imag, constants):
    third_high, third_low = constants.third
    fourth_high, fourth_low = constants.fourth
    high, low = split(jnp.concatenate([real, imag], axis=1))
    stage = mm(high, third_high[...]) + mm(low, third_high[...]) + mm(high, third_low[...])
    half = stage.shape[1] // 2
    real, imag = twiddle(stage[:, :half], stage[:, half:], constants.cosine(), -constants.sine())
    high, low = split(jnp.concatenate([real, imag], axis=0))
    return mm(fourth_high[...], high) + mm(fourth_high[...], low) + mm(fourth_low[...], high)


def spread(values, wide_ref):
    wide_ref[...] = values.reshape(wide_ref.shape)


def group_of(wide_ref, group):
    blocks, _, size, lanes = wide_ref.shape
    return wide_ref[:, group].reshape(blocks * size, lanes)


def joined(wide_ref):
    blocks, groups, size, lanes = wide_ref.shape
    return wide_ref[...].reshape(blocks * groups * size, lanes)


def started(copies):
    for copy in copies:
        copy.start()
    return copies


def onehots(ids_ref, s, chans, vocab):
    quarter = chans // 4
    lanes = ids_ref.shape[1]
    block = ids_ref[pl.ds(pl.multiple_of(s * chans, chans), chans), :]
    block = block.astype(F32)
    labels = lax.broadcasted_iota(jnp.int32, (16, lanes), 0).astype(F32)
    halves = []
    for half in range(2):
        coarse = jnp.broadcast_to(block[half * quarter : half * quarter + 1], (16, lanes))
        fine = block[(2 + half) * quarter : (2 + half) * quarter + 1]
        fine_hot = (labels == fine).astype(F32).astype(BF)
        coarse = coarse.astype(BF)
        zero = jnp.zeros_like(fine_hot)
        halves.append(
            jnp.concatenate(
                [
                    jnp.where(coarse == jnp.array(part, BF), fine_hot, zero)
                    for part in range(vocab // 16)
                ],
                axis=0,
            )
        )
    return jnp.concatenate(halves, axis=1)


def send_kernel(f_ref, ids_ref, out_ref):
    rows, width = f_ref.shape
    out_ref[:, :rows] = f_ref[...].T.astype(BF)
    ids = ids_ref[...]
    coarse = ids // 16
    pieces = (coarse, ids - 16 * coarse)
    lanes = 128
    quarters = [
        jnp.broadcast_to(piece[:, half * lanes : (half + 1) * lanes].astype(F32), (4, lanes))
        for piece in pieces
        for half in range(2)
    ]
    tile = jnp.concatenate(quarters, axis=0).astype(BF)
    for start in range(0, width, 16):
        out_ref[start : start + 16, rows:] = tile


def front_kernel(
    scale, in_ref, tab_ref, constants_hbm, parts_hbm, spectra_hbm, mixed_ref,
    constants_ref, parts_ref, spectra_ref, wide_ref, in_sems, out_sems,
):
    width, rows = mixed_ref.shape
    chans = tab_ref.shape[0] // 3
    vocab = tab_ref.shape[1]
    blocks = width // chans
    half = width // 2
    size = wide_ref.shape[2]
    constants = Constants(constants_ref, blocks, rows)
    total = constants_ref.shape[0]
    incoming = started(
        [
            pltpu.make_async_copy(constants_hbm.at[part], constants_ref.at[part], in_sems.at[place])
            for place, part in enumerate((slice(0, constants.early), slice(constants.early, total)))
        ]
    )
    query, key, value, ids = (slice(rows * part, rows * (part + 1)) for part in range(4))
    ids = slice(3 * rows, parts_ref.shape[1])
    parts_ref[:, ids] = in_ref[:, rows:]

    def body(s, carry):
        picked = mm(tab_ref[...], onehots(in_ref.at[:, rows:], s, chans, vocab)).astype(BF)
        place = pl.ds(pl.multiple_of(s * chans, chans), chans)
        parts_ref[place, query] = picked[:chans]
        parts_ref[place, key] = picked[chans : 2 * chans]
        parts_ref[place, value] = picked[2 * chans :]
        return carry

    lax.fori_loop(0, blocks, body, 0, unroll=8)
    leaving = started([pltpu.make_async_copy(parts_ref, parts_hbm, out_sems.at[0])])
    incoming[0].wait()
    spread(in_ref[:, :rows].astype(F32), wide_ref)
    fr, fi, gr, gi, cause = (slice(rows * part, rows * (part + 1)) for part in range(5))
    for group in range(2):
        place = slice(group * half, (group + 1) * half)
        spectra_ref[place, : 2 * rows] = forward(group_of(wide_ref, group), False, constants) * scale
    spread(parts_ref[:, key].astype(F32) * parts_ref[:, value].astype(F32), wide_ref)
    for group in range(2):
        place = slice(group * half, (group + 1) * half)
        spectra_ref[place, 2 * rows : 4 * rows] = forward(
            group_of(wide_ref, group), True, constants
        )
    leaving += started(
        [
            pltpu.make_async_copy(
                spectra_ref.at[:, : 4 * rows], spectra_hbm.at[:, : 4 * rows], out_sems.at[1]
            )
        ]
    )
    incoming[1].wait()
    for group in range(2):
        place = slice(group * half, (group + 1) * half)
        a, b = spectra_ref[place, fr], spectra_ref[place, fi]
        c, d = spectra_ref[place, gr], spectra_ref[place, gi]
        causal = inverse(c * a - d * b, c * b + d * a, constants)
        wide_ref[:, group] = causal.reshape(blocks, size, rows)
    causal = joined(wide_ref)
    spectra_ref[:, cause] = causal
    leaving += started(
        [
            pltpu.make_async_copy(
                spectra_ref.at[:, cause], spectra_hbm.at[:, cause], out_sems.at[2]
            )
        ]
    )
    mixed_ref[...] = (parts_ref[:, query].astype(F32) * causal).astype(BF)
    for copy in leaving:
        copy.wait()


def back_kernel(
    scale, b_ref, constants_ref, parts_ref, spectra_ref, out_ref,
    act_ref, spec_ref, acc_ref, wide_ref,
):
    width, rows = b_ref.shape
    blocks = act_ref.shape[0]
    chans = width // blocks
    vocab = acc_ref.shape[0]
    half = width // 2
    size = wide_ref.shape[2]
    shape = (blocks, chans, rows)
    constants = Constants(constants_ref, blocks, rows)
    query, key, value = (slice(rows * part, rows * (part + 1)) for part in range(3))
    ids = slice(3 * rows, parts_ref.shape[1])
    spread(b_ref[...].astype(F32) * parts_ref[:, query].astype(F32), wide_ref)
    for group in range(2):
        place = slice(group * half, (group + 1) * half)
        spec_ref[place] = forward(group_of(wide_ref, group), True, constants)

    def correlate(start):
        for group in range(2):
            place = slice(group * half, (group + 1) * half)
            cr, ci = spec_ref[place, :rows], spec_ref[place, rows:]
            xr = spectra_ref[place, start : start + rows]
            xi = spectra_ref[place, start + rows : start + 2 * rows]
            result = inverse(xr * cr + xi * ci, xr * ci - xi * cr, constants)
            wide_ref[:, group] = result.reshape(blocks, size, rows)
        return joined(wide_ref)

    out_ref[:, :rows] = (correlate(2 * rows) * scale).astype(BF)
    causal = spectra_ref[:, 4 * rows :]
    act_ref[:, :chans] = (b_ref[...].astype(F32) * causal).astype(BF).reshape(shape)
    gated_grad = correlate(0)
    act_ref[:, chans : 2 * chans] = (
        (gated_grad * parts_ref[:, value].astype(F32)).astype(BF).reshape(shape)
    )
    act_ref[:, 2 * chans :] = (
        (gated_grad * parts_ref[:, key].astype(F32)).astype(BF).reshape(shape)
    )
    acc_ref[...] = jnp.zeros_like(acc_ref)
    group = 8

    def body(step, carry):
        hot = jnp.concatenate(
            [onehots(parts_ref.at[:, ids], step * group + g, chans, vocab) for g in range(group)],
            axis=1,
        )
        act = jnp.concatenate([act_ref[step * group + g] for g in range(group)], axis=1)
        acc_ref[:, : 3 * chans] += lax.dot_general(
            hot, act, (((1,), (1,)), ((), ())), preferred_element_type=F32
        )
        return carry

    lax.fori_loop(0, blocks // group, body, 0, unroll=blocks // group)
    out_ref[:, rows:] = acc_ref[...].astype(BF)


def finish_kernel(in_ref, grad_ref, table_ref):
    width, rows = grad_ref.shape[1], grad_ref.shape[0]
    vocab_rows = table_ref.shape[1]
    chans = vocab_rows * width // in_ref.shape[0]
    grad_ref[...] = in_ref[:, :rows].astype(F32).T
    sums = in_ref[:, rows:]
    lanes = sums.shape[1]
    column = lax.broadcasted_iota(jnp.int32, (lanes, width), 1)
    row = lax.broadcasted_iota(jnp.int32, (lanes, width), 0)
    source = lax.broadcasted_iota(jnp.int32, (width, width), 0) // vocab_rows
    mine = source == lax.broadcasted_iota(jnp.int32, (width, width), 1) // chans
    pick = lax.broadcasted_iota(jnp.int32, (vocab_rows, width), 1) % vocab_rows
    pick = pick == lax.broadcasted_iota(jnp.int32, (vocab_rows, width), 0)
    pick = pick.astype(F32).astype(BF)
    for field in range(3):
        take = (row == field * chans + column % chans).astype(F32).astype(BF)
        spreaded = jnp.where(mine, mm(sums, take), 0.0).astype(BF)
        table_ref[field] = mm(pick, spreaded)


def params(mebibytes):
    return pltpu.CompilerParams(vmem_limit_bytes=mebibytes * 1024 * 1024)


HBM = pl.BlockSpec(memory_space=pltpu.HBM)
VMEM = pl.BlockSpec(memory_space=pltpu.VMEM)
DMA = pltpu.SemaphoreType.DMA


def shards(token_ids, table, filter_raw, w_out, cotangent):
    rows = token_ids.shape[0]
    blocks = lax.axis_size("ctx")
    width, features = w_out.shape
    chans = width // blocks
    vocab = table.shape[0]
    length = rows * blocks
    position = lax.axis_index("ctx")
    scale = 1.0 / math.sqrt(length)
    constants = tables(blocks, chans // 2, rows)
    struct = jax.ShapeDtypeStruct
    field = struct((width, rows), BF)
    parts = struct((width, 3 * rows + 128), BF)
    spectra = struct((width, 5 * rows), F32)
    parcel = struct((width, rows + 128), BF)
    spread_shape = pltpu.VMEM((blocks, 2, chans // 2, rows), F32)
    chunks = 8
    lanes = features // chunks

    def exchange(values):
        return lax.all_to_all(values, "ctx", split_axis=0, concat_axis=0, tiled=True)

    sent = pl.pallas_call(
        send_kernel, out_shape=parcel, compiler_params=params(62), name="send"
    )(filter_raw, token_ids[None])
    sent, table = lax.optimization_barrier((sent, table))
    local = lax.dynamic_slice(table, (0, 0, position * chans), (vocab, 3, chans))
    local = local.transpose(1, 2, 0).reshape(3 * chans, vocab)
    sent, local = lax.optimization_barrier((sent, local))
    received = exchange(sent)
    cot_full = lax.all_gather(cotangent, "tp", axis=1, tiled=True)

    held, spectra_held, mixed = pl.pallas_call(
        functools.partial(front_kernel, scale),
        out_shape=(parts, spectra, field),
        in_specs=[VMEM, VMEM, HBM],
        out_specs=(HBM, HBM, VMEM),
        scratch_shapes=[
            pltpu.VMEM(constants.shape, BF),
            pltpu.VMEM(parts.shape, BF),
            pltpu.VMEM(spectra.shape, F32),
            spread_shape,
            DMA((2,)),
            DMA((3,)),
        ],
        compiler_params=params(50),
        name="front",
    )(received, local, constants)
    mixed_rows = exchange(mixed)
    partial_out = lax.dot_general(
        mixed_rows, w_out, (((0,), (0,)), ((), ())), preferred_element_type=F32
    ).astype(BF)
    output = lax.psum_scatter(partial_out, "tp", scatter_dimension=1, tiled=True)

    back = lax.dot_general(
        w_out, cot_full, (((1,), (1,)), ((), ())), preferred_element_type=F32
    ).astype(BF)
    back_field = exchange(back)
    grads = pl.pallas_call(
        functools.partial(back_kernel, scale),
        out_shape=parcel,
        scratch_shapes=[
            pltpu.VMEM((blocks, 3 * chans, rows), BF),
            pltpu.VMEM((width, 2 * rows), F32),
            pltpu.VMEM((vocab, 128), F32),
            spread_shape,
        ],
        compiler_params=params(24),
        name="back",
    )(back_field, constants, held, spectra_held)
    grads = exchange(grads)
    vocab_rows = vocab // blocks
    grad_filter, grad_table = pl.pallas_call(
        finish_kernel,
        out_shape=(struct((rows, width), F32), struct((3, vocab_rows, width), F32)),
        compiler_params=params(8),
        name="finish",
    )(grads)
    return (output, grad_filter, grad_table.transpose(1, 0, 2))


def solution(mesh):
    return jax.shard_map(
        shards,
        mesh=mesh,
        in_specs=(P("ctx"), P(None, None, "tp"), P("ctx", "tp"), P("tp", None), P("ctx", "tp")),
        out_specs=(P("ctx", "tp"), P("ctx", "tp"), P("ctx", None, "tp")),
        check_vma=False,
    )
```

```python
import functools
import math

import jax
import jax.numpy as jnp
import ml_dtypes
import numpy as np
from jax import lax
from jax.experimental import pallas as pl
from jax.experimental.pallas import tpu as pltpu
from jax.sharding import PartitionSpec as P

BF = jnp.bfloat16
F32 = jnp.float32


def split_np(values):
    high = values.astype(np.float32).astype(ml_dtypes.bfloat16)
    low = (values - high.astype(np.float64)).astype(np.float32).astype(ml_dtypes.bfloat16)
    return high, low


@functools.lru_cache(maxsize=None)
def tables(blocks, chans, rows):
    period = 2 * blocks * rows
    s = np.arange(blocks, dtype=np.float64)
    r = np.arange(rows, dtype=np.float64)
    odd = np.arange(blocks, dtype=np.float64) + 0.5
    outer = 2 * np.pi * odd[:, None] * s[None, :] / (2 * blocks)
    eye = np.eye(chans)
    real = np.einsum("ks,cd->cksd", np.cos(outer), eye).reshape(chans * blocks, blocks * chans)
    imag = np.einsum("ks,cd->cksd", -np.sin(outer), eye).reshape(chans * blocks, blocks * chans)
    first = np.concatenate([real, imag], axis=0)
    inner = 2 * np.pi * (np.outer(r, r) % rows) / rows
    cosine, sine = np.cos(inner), np.sin(inner)
    second = np.block([[cosine, -sine], [sine, cosine]])
    twist = 2 * np.pi * odd[:, None] * r[None, :] / period
    return np.concatenate(
        [
            np.concatenate(split_np(np.cos(twist)), axis=1),
            np.concatenate(split_np(np.sin(twist)), axis=1),
            np.concatenate(split_np(first), axis=1),
            *split_np(second),
            *split_np(second.T.copy()),
            *split_np(first.T * (2.0 / period)),
        ],
        axis=0,
    )


class Constants:
    def __init__(self, ref, blocks, rows):
        inner = ref.shape[1]
        start = 0

        def take(count):
            nonlocal start
            start += count
            return slice(start - count, start)

        cosine, sine, first = take(blocks), take(blocks), take(2 * rows)
        high, low = slice(0, rows), slice(rows, 2 * rows)
        self.cosine = lambda: ref[cosine, high].astype(F32) + ref[cosine, low].astype(F32)
        self.sine = lambda: ref[sine, high].astype(F32) + ref[sine, low].astype(F32)
        self.first = (ref.at[first, high], ref.at[first, low])
        self.second = (ref.at[take(inner)], ref.at[take(inner)])
        self.early = start
        self.third = (ref.at[take(inner)], ref.at[take(inner)])
        self.fourth = (ref.at[take(rows)], ref.at[take(rows)])


def split(values):
    high = values.astype(BF)
    return high, (values - high.astype(F32)).astype(BF)


def mm(left, right):
    return jnp.dot(left, right, preferred_element_type=F32)


def twiddle(real, imag, cosine, sine):
    rows, lanes = real.shape
    blocks = cosine.shape[0]
    shape = (rows // blocks, blocks, lanes)
    cosine = cosine[None]
    sine = sine[None]
    real = real.reshape(shape)
    imag = imag.reshape(shape)
    return (
        (real * cosine + imag * sine).reshape(rows, lanes),
        (imag * cosine - real * sine).reshape(rows, lanes),
    )


def forward(values, low_too, constants):
    first_high, first_low = constants.first
    second_high, second_low = constants.second
    high, low = split(values)
    stage = mm(first_high[...], high) + mm(first_low[...], high)
    if low_too:
        stage = stage + mm(first_high[...], low)
    half = stage.shape[0] // 2
    real, imag = twiddle(stage[:half], stage[half:], constants.cosine(), constants.sine())
    high, low = split(jnp.concatenate([real, imag], axis=1))
    return mm(high, second_high[...]) + mm(low, second_high[...]) + mm(high, second_low[...])


def inverse(real, imag, constants):
    third_high, third_low = constants.third
    fourth_high, fourth_low = constants.fourth
    high, low = split(jnp.concatenate([real, imag], axis=1))
    stage = mm(high, third_high[...]) + mm(low, third_high[...]) + mm(high, third_low[...])
    half = stage.shape[1] // 2
    real, imag = twiddle(stage[:, :half], stage[:, half:], constants.cosine(), -constants.sine())
    high, low = split(jnp.concatenate([real, imag], axis=0))
    return mm(fourth_high[...], high) + mm(fourth_high[...], low) + mm(fourth_low[...], high)


def spread(values, wide_ref):
    wide_ref[...] = values.reshape(wide_ref.shape)


def group_of(wide_ref, group):
    blocks, _, size, lanes = wide_ref.shape
    return wide_ref[:, group].reshape(blocks * size, lanes)


def joined(wide_ref):
    blocks, groups, size, lanes = wide_ref.shape
    return wide_ref[...].reshape(blocks * groups * size, lanes)


def started(copies):
    for copy in copies:
        copy.start()
    return copies


def onehots(ids_ref, s, chans, vocab):
    quarter = chans // 4
    lanes = ids_ref.shape[1]
    block = ids_ref[pl.ds(pl.multiple_of(s * chans, chans), chans), :]
    block = block.astype(F32)
    labels = lax.broadcasted_iota(jnp.int32, (16, lanes), 0).astype(F32)
    halves = []
    for half in range(2):
        coarse = jnp.broadcast_to(block[half * quarter : half * quarter + 1], (16, lanes))
        fine = block[(2 + half) * quarter : (2 + half) * quarter + 1]
        fine_hot = (labels == fine).astype(F32).astype(BF)
        coarse = coarse.astype(BF)
        zero = jnp.zeros_like(fine_hot)
        halves.append(
            jnp.concatenate(
                [
                    jnp.where(coarse == jnp.array(part, BF), fine_hot, zero)
                    for part in range(vocab // 16)
                ],
                axis=0,
            )
        )
    return jnp.concatenate(halves, axis=1)


def send_kernel(f_ref, ids_ref, out_ref):
    rows, width = f_ref.shape
    out_ref[:, :rows] = f_ref[...].T.astype(BF)
    ids = ids_ref[...]
    coarse = ids // 16
    pieces = (coarse, ids - 16 * coarse)
    lanes = 128
    quarters = [
        jnp.broadcast_to(piece[:, half * lanes : (half + 1) * lanes].astype(F32), (4, lanes))
        for piece in pieces
        for half in range(2)
    ]
    tile = jnp.concatenate(quarters, axis=0).astype(BF)
    for start in range(0, width, 16):
        out_ref[start : start + 16, rows:] = tile


def front_kernel(
    scale, in_ref, tab_ref, constants_hbm, parts_hbm, spectra_hbm, mixed_ref,
    constants_ref, parts_ref, spectra_ref, wide_ref, in_sems, out_sems,
):
    width, rows = mixed_ref.shape
    chans = tab_ref.shape[0] // 3
    vocab = tab_ref.shape[1]
    blocks = width // chans
    half = width // 2
    size = wide_ref.shape[2]
    constants = Constants(constants_ref, blocks, rows)
    total = constants_ref.shape[0]
    incoming = started(
        [
            pltpu.make_async_copy(constants_hbm.at[part], constants_ref.at[part], in_sems.at[place])
            for place, part in enumerate((slice(0, constants.early), slice(constants.early, total)))
        ]
    )
    query, key, value, ids = (slice(rows * part, rows * (part + 1)) for part in range(4))
    ids = slice(3 * rows, parts_ref.shape[1])
    parts_ref[:, ids] = in_ref[:, rows:]

    def body(s, carry):
        picked = mm(tab_ref[...], onehots(in_ref.at[:, rows:], s, chans, vocab)).astype(BF)
        place = pl.ds(pl.multiple_of(s * chans, chans), chans)
        parts_ref[place, query] = picked[:chans]
        parts_ref[place, key] = picked[chans : 2 * chans]
        parts_ref[place, value] = picked[2 * chans :]
        return carry

    lax.fori_loop(0, blocks, body, 0, unroll=8)
    leaving = started([pltpu.make_async_copy(parts_ref, parts_hbm, out_sems.at[0])])
    incoming[0].wait()
    spread(in_ref[:, :rows].astype(F32), wide_ref)
    fr, fi, gr, gi, cause = (slice(rows * part, rows * (part + 1)) for part in range(5))
    for group in range(2):
        place = slice(group * half, (group + 1) * half)
        spectra_ref[place, : 2 * rows] = forward(group_of(wide_ref, group), False, constants) * scale
    spread(parts_ref[:, key].astype(F32) * parts_ref[:, value].astype(F32), wide_ref)
    for group in range(2):
        place = slice(group * half, (group + 1) * half)
        spectra_ref[place, 2 * rows : 4 * rows] = forward(
            group_of(wide_ref, group), True, constants
        )
    leaving += started(
        [
            pltpu.make_async_copy(
                spectra_ref.at[:, : 4 * rows], spectra_hbm.at[:, : 4 * rows], out_sems.at[1]
            )
        ]
    )
    incoming[1].wait()
    for group in range(2):
        place = slice(group * half, (group + 1) * half)
        a, b = spectra_ref[place, fr], spectra_ref[place, fi]
        c, d = spectra_ref[place, gr], spectra_ref[place, gi]
        causal = inverse(c * a - d * b, c * b + d * a, constants)
        wide_ref[:, group] = causal.reshape(blocks, size, rows)
    causal = joined(wide_ref)
    spectra_ref[:, cause] = causal
    leaving += started(
        [
            pltpu.make_async_copy(
                spectra_ref.at[:, cause], spectra_hbm.at[:, cause], out_sems.at[2]
            )
        ]
    )
    mixed_ref[...] = (parts_ref[:, query].astype(F32) * causal).astype(BF)
    for copy in leaving:
        copy.wait()


def back_kernel(
    scale, b_ref, constants_ref, parts_ref, spectra_ref, out_ref,
    act_ref, spec_ref, acc_ref, wide_ref,
):
    width, rows = b_ref.shape
    blocks = act_ref.shape[0]
    chans = width // blocks
    vocab = acc_ref.shape[0]
    half = width // 2
    size = wide_ref.shape[2]
    shape = (blocks, chans, rows)
    constants = Constants(constants_ref, blocks, rows)
    query, key, value = (slice(rows * part, rows * (part + 1)) for part in range(3))
    ids = slice(3 * rows, parts_ref.shape[1])
    spread(b_ref[...].astype(F32) * parts_ref[:, query].astype(F32), wide_ref)
    for group in range(2):
        place = slice(group * half, (group + 1) * half)
        spec_ref[place] = forward(group_of(wide_ref, group), True, constants)

    def correlate(start):
        for group in range(2):
            place = slice(group * half, (group + 1) * half)
            cr, ci = spec_ref[place, :rows], spec_ref[place, rows:]
            xr = spectra_ref[place, start : start + rows]
            xi = spectra_ref[place, start + rows : start + 2 * rows]
            result = inverse(xr * cr + xi * ci, xr * ci - xi * cr, constants)
            wide_ref[:, group] = result.reshape(blocks, size, rows)
        return joined(wide_ref)

    out_ref[:, :rows] = (correlate(2 * rows) * scale).astype(BF)
    causal = spectra_ref[:, 4 * rows :]
    act_ref[:, :chans] = (b_ref[...].astype(F32) * causal).astype(BF).reshape(shape)
    gated_grad = correlate(0)
    act_ref[:, chans : 2 * chans] = (
        (gated_grad * parts_ref[:, value].astype(F32)).astype(BF).reshape(shape)
    )
    act_ref[:, 2 * chans :] = (
        (gated_grad * parts_ref[:, key].astype(F32)).astype(BF).reshape(shape)
    )
    acc_ref[...] = jnp.zeros_like(acc_ref)
    group = 16

    def body(step, carry):
        hot = jnp.concatenate(
            [onehots(parts_ref.at[:, ids], step * group + g, chans, vocab) for g in range(group)],
            axis=1,
        )
        act = jnp.concatenate([act_ref[step * group + g] for g in range(group)], axis=1)
        acc_ref[:, : 3 * chans] += lax.dot_general(
            hot, act, (((1,), (1,)), ((), ())), preferred_element_type=F32
        )
        return carry

    lax.fori_loop(0, blocks // group, body, 0, unroll=blocks // group)
    out_ref[:, rows:] = acc_ref[...].astype(BF)


def finish_kernel(in_ref, grad_ref, table_ref):
    width, rows = grad_ref.shape[1], grad_ref.shape[0]
    vocab_rows = table_ref.shape[1]
    chans = vocab_rows * width // in_ref.shape[0]
    grad_ref[...] = in_ref[:, :rows].astype(F32).T
    sums = in_ref[:, rows:]
    lanes = sums.shape[1]
    column = lax.broadcasted_iota(jnp.int32, (lanes, width), 1)
    row = lax.broadcasted_iota(jnp.int32, (lanes, width), 0)
    source = lax.broadcasted_iota(jnp.int32, (width, width), 0) // vocab_rows
    mine = source == lax.broadcasted_iota(jnp.int32, (width, width), 1) // chans
    pick = lax.broadcasted_iota(jnp.int32, (vocab_rows, width), 1) % vocab_rows
    pick = pick == lax.broadcasted_iota(jnp.int32, (vocab_rows, width), 0)
    pick = pick.astype(F32).astype(BF)
    for field in range(3):
        take = (row == field * chans + column % chans).astype(F32).astype(BF)
        spreaded = jnp.where(mine, mm(sums, take), 0.0).astype(BF)
        table_ref[field] = mm(pick, spreaded)


def params(mebibytes):
    return pltpu.CompilerParams(vmem_limit_bytes=mebibytes * 1024 * 1024)


HBM = pl.BlockSpec(memory_space=pltpu.HBM)
VMEM = pl.BlockSpec(memory_space=pltpu.VMEM)
DMA = pltpu.SemaphoreType.DMA


def shards(token_ids, table, filter_raw, w_out, cotangent):
    rows = token_ids.shape[0]
    blocks = lax.axis_size("ctx")
    width, features = w_out.shape
    chans = width // blocks
    vocab = table.shape[0]
    length = rows * blocks
    position = lax.axis_index("ctx")
    scale = 1.0 / math.sqrt(length)
    constants = tables(blocks, chans // 2, rows)
    struct = jax.ShapeDtypeStruct
    field = struct((width, rows), BF)
    parts = struct((width, 3 * rows + 128), BF)
    spectra = struct((width, 5 * rows), F32)
    parcel = struct((width, rows + 128), BF)
    spread_shape = pltpu.VMEM((blocks, 2, chans // 2, rows), F32)
    chunks = 8
    lanes = features // chunks

    def exchange(values):
        return lax.all_to_all(values, "ctx", split_axis=0, concat_axis=0, tiled=True)

    sent = pl.pallas_call(
        send_kernel, out_shape=parcel, compiler_params=params(62), name="send"
    )(filter_raw, token_ids[None])
    sent, table = lax.optimization_barrier((sent, table))
    local = lax.dynamic_slice(table, (0, 0, position * chans), (vocab, 3, chans))
    local = local.transpose(1, 2, 0).reshape(3 * chans, vocab)
    sent, local = lax.optimization_barrier((sent, local))
    received = exchange(sent)
    cot_full = lax.all_gather(cotangent, "tp", axis=1, tiled=True)

    held, spectra_held, mixed = pl.pallas_call(
        functools.partial(front_kernel, scale),
        out_shape=(parts, spectra, field),
        in_specs=[VMEM, VMEM, HBM],
        out_specs=(HBM, HBM, VMEM),
        scratch_shapes=[
            pltpu.VMEM(constants.shape, BF),
            pltpu.VMEM(parts.shape, BF),
            pltpu.VMEM(spectra.shape, F32),
            spread_shape,
            DMA((2,)),
            DMA((3,)),
        ],
        compiler_params=params(50),
        name="front",
    )(received, local, constants)
    mixed_rows = exchange(mixed)
    partial_out = lax.dot_general(
        mixed_rows, w_out, (((0,), (0,)), ((), ())), preferred_element_type=F32
    ).astype(BF)
    output = lax.psum_scatter(partial_out, "tp", scatter_dimension=1, tiled=True)

    back = lax.dot_general(
        w_out, cot_full, (((1,), (1,)), ((), ())), preferred_element_type=F32
    ).astype(BF)
    back_field = exchange(back)
    grads = pl.pallas_call(
        functools.partial(back_kernel, scale),
        out_shape=parcel,
        scratch_shapes=[
            pltpu.VMEM((blocks, 3 * chans, rows), BF),
            pltpu.VMEM((width, 2 * rows), F32),
            pltpu.VMEM((vocab, 128), F32),
            spread_shape,
        ],
        compiler_params=params(24),
        name="back",
    )(back_field, constants, held, spectra_held)
    grads = exchange(grads)
    vocab_rows = vocab // blocks
    grad_filter, grad_table = pl.pallas_call(
        finish_kernel,
        out_shape=(struct((rows, width), F32), struct((3, vocab_rows, width), F32)),
        compiler_params=params(8),
        name="finish",
    )(grads)
    return (output, grad_filter, grad_table.transpose(1, 0, 2))


def solution(mesh):
    return jax.shard_map(
        shards,
        mesh=mesh,
        in_specs=(P("ctx"), P(None, None, "tp"), P("ctx", "tp"), P("tp", None), P("ctx", "tp")),
        out_specs=(P("ctx", "tp"), P("ctx", "tp"), P("ctx", None, "tp")),
        check_vma=False,
    )
```
